256 devices in a mesh: dp: 8 (over y, core), ctx: 32 (over z, x).
Axes of the slice: x: 4, y: 4, z: 8, core: 2. Of those that a mesh axis runs over, the one named last changes fastest.
Arguments:
- inputs: bfloat16 [8, 8192, 2048], P('dp', 'ctx'), may hold values from -6 to 6
- grad_out: bfloat16 [8, 8192, 2048], P('dp', 'ctx'), may hold values from -6 to 6
- w_first: float32 [64, 33], replicated, may hold values from -1 to 1
- b_first: float32 [64], replicated, may hold values from -4 to 4
- w_mid: float32 [64, 64], replicated, may hold values from -0.75 to 0.75
- b_mid: float32 [64], replicated, may hold values from -4 to 4
- w_last: float32 [2048, 64], replicated, may hold values from -0.75 to 0.75
- decay_rate: float32 [2048], replicated, may hold values from 0.5 to 19.2
Outputs:
- clip_first: float32 [64, 33], replicated
- clip_first_bias: float32 [64], replicated
- clip_mid: float32 [64, 64], replicated
- clip_mid_bias: float32 [64], replicated
- clip_last: float32 [2048, 64], replicated
The draws below stay inside these ranges and needn't reach their ends.
All inputs are finite; a program needn't handle non-finite values.
Results may differ from the reference program's by a relative error of at most 0.0052.
Values may be sent and summed in bfloat16 or wider, within the bound.
A program may use at most 128 MiB of HBM per device.

```python
import math
import jax
import jax.numpy as jnp
from jax import lax

CH = 2048
ORDER = 64
BANDS = 16
FB = 256
EMB = 33
FA = 32
SEQ_LEN = 8192
BATCH = 8


def levels(rng, extent, split, low, largest):
    level, own = 1.0, jax.random.fold_in(rng, 6)
    for position, blocks in split:
        steps = jnp.exp(jax.random.uniform(jax.random.fold_in(own, position), (blocks,), jnp.float32, low / len(split), largest / len(split)))
        level = level * jnp.repeat(steps, extent[position] // blocks).reshape([-1 if axis == position else 1 for axis in range(len(extent))])
    return level


def noise(own_key, extent, deviation, bound, pieces=(), held_as=jnp.bfloat16):
    drawn = jax.random.normal(own_key, extent, jnp.float32) * deviation
    if len(pieces) > 0:
        drawn = levels(own_key, extent, pieces, -0.22, 0.18) * drawn
    return jnp.clip(drawn, min=-bound, max=bound).astype(held_as)


def setup_inputs(seed: int = 0) -> dict:
    splits = jax.random.split(jax.random.key(seed), 9)
    return {
        "inputs": noise(splits[0], (BATCH, SEQ_LEN, CH), 1.0, 6.0, ((0, 8), (1, 32))),
        "grad_out": noise(splits[1], (BATCH, SEQ_LEN, CH), 1.0, 6.0, ((0, 8), (1, 32))),
        "w_first": noise(splits[2], (ORDER, EMB), EMB ** -0.5, 1.0, (), jnp.float32),
        "b_first": noise(splits[3], (ORDER,), 1.0, 4.0, (), jnp.float32),
        "w_mid": noise(splits[4], (ORDER, ORDER), ORDER ** -0.5, 0.75, (), jnp.float32),
        "b_mid": noise(splits[5], (ORDER,), 1.0, 4.0, (), jnp.float32),
        "w_last": noise(splits[6], (CH, ORDER), ORDER ** -0.5, 0.75, (), jnp.float32),
        "decay_rate": jnp.clip(jnp.exp(jax.random.uniform(splits[7], (CH,), jnp.float32, math.log(0.5), math.log(19.2))), 0.5, 19.2),
    }


def mix(form, left, right):
    return jnp.einsum(form, left.astype(jnp.float32), right.astype(jnp.float32), precision=lax.Precision.HIGHEST)

def dense(left, right):
    return jnp.dot(left, right, precision=lax.Precision.HIGHEST)

def dft_tables(rows_all, cols_all):
    twice_ids = jnp.arange(2 * rows_all, dtype=jnp.int32)[:, None]
    row_ids = jnp.arange(rows_all, dtype=jnp.int32)[None, :]
    angle_rows = math.pi * (twice_ids * row_ids % (2 * rows_all)).astype(jnp.float32) / rows_all
    col_ids = jnp.arange(cols_all, dtype=jnp.int32)
    angle_cols = 2.0 * math.pi * (col_ids[:, None] * col_ids[None, :] % cols_all).astype(jnp.float32) / cols_all
    return (jnp.cos(angle_rows).astype(jnp.bfloat16), (-jnp.sin(angle_rows)).astype(jnp.bfloat16), jnp.cos(angle_cols).astype(jnp.bfloat16), (-jnp.sin(angle_cols)).astype(jnp.bfloat16))

def twiddle(freq_ids, col_ids, seq_len):
    angle = math.pi * (freq_ids[:, None] * col_ids[None, :] % (2 * seq_len)).astype(jnp.float32) / seq_len
    return (jnp.cos(angle), -jnp.sin(angle))

def section_forward(stacked_pair, tables, col_ids, seq_len):
    first_re, first_im, second_re, second_im = tables
    part_re = mix('jn,vnmc->vjmc', first_re, stacked_pair)
    part_im = mix('jn,vnmc->vjmc', first_im, stacked_pair)
    turn_re, turn_im = twiddle(jnp.arange(first_re.shape[0], dtype=jnp.int32), col_ids, seq_len)
    turn_re = turn_re[None, :, :, None]
    turn_im = turn_im[None, :, :, None]
    out_re = part_re * turn_re - part_im * turn_im
    out_im = part_re * turn_im + part_im * turn_re
    stacked = jnp.stack([out_re, out_im], axis=1)
    return stacked.reshape((4,) + out_re.shape[1:]).astype(jnp.bfloat16)

def section_cross(spectra, tables, freq_ids, seq_len):
    first_re, first_im, second_re, second_im = tables
    with_re = mix('kn,sjnc->sjkc', second_re, spectra)
    with_im = mix('kn,sjnc->sjkc', second_im, spectra)
    input_re = with_re[0] - with_im[1]
    input_im = with_re[1] + with_im[0]
    grad_re = with_re[2] - with_im[3]
    grad_im = with_re[3] + with_im[2]
    cross = jnp.stack([input_re * grad_re + input_im * grad_im, input_re * grad_im - input_im * grad_re]).astype(jnp.bfloat16)
    back_re = mix('tk,sjkc->sjtc', second_re, cross)
    back_im = mix('tk,sjkc->sjtc', second_im, cross)
    inner_re = back_re[0] + back_im[1]
    inner_im = back_re[1] - back_im[0]
    turn_re, turn_im = twiddle(freq_ids, jnp.arange(second_re.shape[0], dtype=jnp.int32), seq_len)
    turn_re = turn_re[:, :, None]
    turn_im = turn_im[:, :, None]
    out_re = inner_re * turn_re + inner_im * turn_im
    out_im = inner_im * turn_re - inner_re * turn_im
    return jnp.stack([out_re, out_im]).astype(jnp.bfloat16)

def section_inverse(returned, tables, seq_len):
    first_re, first_im, second_re, second_im = tables
    summed = mix('jt,jmc->tmc', first_re, returned[0]) + mix('jt,jmc->tmc', first_im, returned[1])
    return summed * (0.5 / seq_len)

def features_of(places, seq_len, bands):
    band_ids = jnp.arange(1, bands + 1, dtype=jnp.int32)[:, None]
    angle = 2.0 * math.pi * (band_ids * places[None, :] % seq_len).astype(jnp.float32) / seq_len
    ramp = places[None, :].astype(jnp.float32) / seq_len
    return jnp.concatenate([ramp, jnp.cos(angle), jnp.sin(angle)], axis=0)

def hidden_forward(places, seq_len, bands, w_first, b_first, w_mid, b_mid):
    feats = features_of(places, seq_len, bands)
    pre_first = dense(w_first, feats) + b_first[:, None]
    act_first = jnp.sin(pre_first)
    pre_second = dense(w_mid, act_first) + b_mid[:, None]
    act_second = jnp.sin(pre_second)
    return (feats, pre_first, act_first, pre_second, act_second)

def hidden_backward(d_second, feats, pre_first, act_first, pre_second, w_mid):
    d_pre_second = d_second * jnp.cos(pre_second)
    grad_mid = dense(d_pre_second, act_first.T)
    grad_mid_bias = lax.optimization_barrier(jnp.sum(d_pre_second, axis=1))
    d_pre_first = dense(w_mid.T, d_pre_second) * jnp.cos(pre_first)
    grad_first = dense(d_pre_first, feats.T)
    grad_first_bias = lax.optimization_barrier(jnp.sum(d_pre_first, axis=1))
    return (grad_first, grad_first_bias, grad_mid, grad_mid_bias)

def modulation(places, rates, seq_len):
    return jnp.exp(-rates[None, :] * places[:, None].astype(jnp.float32) / seq_len)

def clip_all(grads):
    squares = sum((jnp.sum(item * item) for item in grads))
    limit = math.sqrt(sum((item.size for item in grads)))
    factor = jnp.minimum(1.0, limit / (jnp.sqrt(squares) + 1e-06))
    return tuple((item * factor for item in grads))

def reference(inputs, grad_out, w_first, b_first, w_mid, b_mid, w_last, decay_rate):
    seq_len = FA * FB
    tables = dft_tables(FA, FB)
    block = 256 if CH % 256 == 0 else CH
    count = CH // block
    col_ids = jnp.arange(FB, dtype=jnp.int32)
    freq_ids = jnp.arange(2 * FA, dtype=jnp.int32)

    def one_block(stacked_pair):
        spectra = section_forward(stacked_pair, tables, col_ids, seq_len)
        returned = section_cross(spectra, tables, freq_ids, seq_len)
        return section_inverse(returned, tables, seq_len)

    def one_sequence(total, sequence):
        blocks = sequence.reshape(2, FA, FB, count, block).transpose(3, 0, 1, 2, 4)
        result = lax.map(one_block, blocks)
        return (total + result.transpose(1, 2, 0, 3).reshape(seq_len, CH), None)
    sequences = jnp.stack([inputs, grad_out], axis=1)
    filter_grad, unused = lax.scan(one_sequence, jnp.zeros((seq_len, CH), jnp.float32), sequences)
    places = jnp.arange(seq_len, dtype=jnp.int32)
    feats, pre_first, act_first, pre_second, act_second = hidden_forward(places, seq_len, BANDS, w_first, b_first, w_mid, b_mid)
    shaped = filter_grad * modulation(places, decay_rate, seq_len)
    grad_last = mix('tc,ot->co', shaped, act_second)
    d_second = mix('co,tc->ot', w_last, shaped)
    small = hidden_backward(d_second, feats, pre_first, act_first, pre_second, w_mid)
    clip_first, clip_first_bias, clip_mid, clip_mid_bias, clip_last = clip_all(small + (grad_last,))
    return (clip_first, clip_first_bias, clip_mid, clip_mid_bias, clip_last)
```

```python
import math

import jax
import jax.numpy as jnp
from jax import lax
from jax.sharding import PartitionSpec as P

BANDS = 16
FB = 256


def mix(form, left, right):
    return jnp.einsum(form, left, right, preferred_element_type=jnp.float32)


def exact(form, left, right):
    return jnp.einsum(form, left, right, precision=lax.Precision.HIGHEST)


def dense(left, right):
    return jnp.dot(left, right, precision=lax.Precision.HIGHEST)


def dft_tables(rows_all, cols_all):
    twice_ids = jnp.arange(rows_all + 1, dtype=jnp.int32)[:, None]
    row_ids = jnp.arange(rows_all, dtype=jnp.int32)[None, :]
    angle_rows = math.pi * (twice_ids * row_ids % (2 * rows_all)).astype(jnp.float32) / rows_all
    col_ids = jnp.arange(cols_all, dtype=jnp.int32)
    angle_cols = (
        2.0
        * math.pi
        * (col_ids[:, None] * col_ids[None, :] % cols_all).astype(jnp.float32)
        / cols_all
    )
    return (
        jnp.cos(angle_rows).astype(jnp.bfloat16),
        (-jnp.sin(angle_rows)).astype(jnp.bfloat16),
        jnp.cos(angle_cols).astype(jnp.bfloat16),
        (-jnp.sin(angle_cols)).astype(jnp.bfloat16),
    )


def twiddle(freq_ids, col_ids, seq_len):
    angle = (
        math.pi
        * (freq_ids[:, None] * col_ids[None, :] % (2 * seq_len)).astype(jnp.float32)
        / seq_len
    )
    return (jnp.cos(angle), -jnp.sin(angle))


def section_forward(stacked_pair, tables, col_ids, seq_len):
    first_re, first_im, second_re, second_im = tables
    part_re = mix("jn,vnmc->vjmc", first_re, stacked_pair)
    part_im = mix("jn,vnmc->vjmc", first_im, stacked_pair)
    turn_re, turn_im = twiddle(jnp.arange(first_re.shape[0], dtype=jnp.int32), col_ids, seq_len)
    turn_re = turn_re[None, :, :, None]
    turn_im = turn_im[None, :, :, None]
    out_re = part_re * turn_re - part_im * turn_im
    out_im = part_re * turn_im + part_im * turn_re
    stacked = jnp.stack([out_re, out_im], axis=1)
    return stacked.reshape((4,) + out_re.shape[1:]).astype(jnp.bfloat16)


def section_cross(spectra, tables, freq_ids, seq_len):
    first_re, first_im, second_re, second_im = tables
    with_re = mix("kn,sjnc->sjkc", second_re, spectra)
    with_im = mix("kn,sjnc->sjkc", second_im, spectra)
    input_re = with_re[0] - with_im[1]
    input_im = with_re[1] + with_im[0]
    grad_re = with_re[2] - with_im[3]
    grad_im = with_re[3] + with_im[2]
    cross = jnp.stack(
        [input_re * grad_re + input_im * grad_im, input_re * grad_im - input_im * grad_re]
    ).astype(jnp.bfloat16)
    back_re = mix("tk,sjkc->sjtc", second_re, cross)
    back_im = mix("tk,sjkc->sjtc", second_im, cross)
    inner_re = back_re[0] + back_im[1]
    inner_im = back_re[1] - back_im[0]
    turn_re, turn_im = twiddle(freq_ids, jnp.arange(second_re.shape[0], dtype=jnp.int32), seq_len)
    turn_re = turn_re[:, :, None]
    turn_im = turn_im[:, :, None]
    out_re = inner_re * turn_re + inner_im * turn_im
    out_im = inner_im * turn_re - inner_re * turn_im
    return jnp.stack([out_re, out_im]).astype(jnp.bfloat16)


def section_inverse(returned, tables, seq_len):
    first_re, first_im, second_re, second_im = tables
    last = first_re.shape[0] - 1
    twice = jnp.where((jnp.arange(last + 1) % last == 0)[:, None], 1.0, 2.0).astype(jnp.bfloat16)
    summed = mix("jt,jmc->tmc", first_re * twice, returned[0]) + mix(
        "jt,jmc->tmc", first_im * twice, returned[1]
    )
    return summed * (0.5 / seq_len)


def features_of(places, seq_len, bands):
    band_ids = jnp.arange(1, bands + 1, dtype=jnp.int32)[:, None]
    angle = 2.0 * math.pi * (band_ids * places[None, :] % seq_len).astype(jnp.float32) / seq_len
    ramp = places[None, :].astype(jnp.float32) / seq_len
    return jnp.concatenate([ramp, jnp.cos(angle), jnp.sin(angle)], axis=0)


def hidden_forward(places, seq_len, bands, w_first, b_first, w_mid, b_mid):
    feats = features_of(places, seq_len, bands)
    pre_first = dense(w_first, feats) + b_first[:, None]
    act_first = jnp.sin(pre_first)
    pre_second = dense(w_mid, act_first) + b_mid[:, None]
    act_second = jnp.sin(pre_second)
    return (feats, pre_first, act_first, pre_second, act_second)


def hidden_backward(d_second, feats, pre_first, act_first, pre_second, w_mid):
    d_pre_second = d_second * jnp.cos(pre_second)
    grad_mid = dense(d_pre_second, act_first.T)
    grad_mid_bias = jnp.sum(d_pre_second, axis=1)
    d_pre_first = dense(w_mid.T, d_pre_second) * jnp.cos(pre_first)
    grad_first = dense(d_pre_first, feats.T)
    grad_first_bias = jnp.sum(d_pre_first, axis=1)
    return (grad_first, grad_first_bias, grad_mid, grad_mid_bias)


def modulation(places, rates, seq_len):
    return jnp.exp(-rates[None, :] * places[:, None].astype(jnp.float32) / seq_len)


def clip_factor(squares, param_count):
    return jnp.minimum(1.0, math.sqrt(param_count) / (jnp.sqrt(squares) + 1e-06))


def clip_all(grads):
    squares = sum((jnp.sum(item * item) for item in grads))
    factor = clip_factor(squares, sum((item.size for item in grads)))
    return tuple((item * factor for item in grads))


def on_device(inputs, grad_out, w_first, b_first, w_mid, b_mid, w_last, decay_rate):
    parts = lax.axis_size("ctx")
    index = lax.axis_index("ctx")
    seq_dev = inputs.shape[1]
    channels = inputs.shape[2]
    rows_dev = seq_dev // FB
    rows_all = rows_dev * parts
    seq_len = rows_all * FB
    tables = dft_tables(rows_all, FB)
    stacked_pair = jnp.stack([inputs[0], grad_out[0]])
    slice_width = channels // parts
    columns = lax.all_to_all(stacked_pair, "ctx", split_axis=2, concat_axis=1, tiled=True)
    blocks = columns.reshape(2, rows_all, FB, slice_width)
    spectra = section_forward(blocks, tables, jnp.arange(FB, dtype=jnp.int32), seq_len)
    returned = section_cross(spectra, tables, jnp.arange(rows_all + 1, dtype=jnp.int32), seq_len)
    filter_grad = section_inverse(returned, tables, seq_len).reshape(seq_len, slice_width)
    start = index * slice_width
    rates = lax.dynamic_slice_in_dim(decay_rate, start, slice_width, 0)
    last_rows = lax.dynamic_slice_in_dim(w_last, start, slice_width, 0)
    places = jnp.arange(seq_len, dtype=jnp.int32)
    feats, pre_first, act_first, pre_second, act_second = hidden_forward(
        places, seq_len, BANDS, w_first, b_first, w_mid, b_mid
    )
    shaped = filter_grad * modulation(places, rates, seq_len)
    last_slice = exact("tc,ot->co", shaped, act_second)
    d_second = exact("co,tc->ot", last_rows, shaped)
    small_part = hidden_backward(d_second, feats, pre_first, act_first, pre_second, w_mid)
    small = lax.psum((small_part[0], small_part[1], small_part[2], small_part[3]), ("dp", "ctx"))
    last_data = lax.psum(last_slice, "dp")
    full_last = lax.all_gather(last_data, "ctx", axis=0, tiled=True)
    results = clip_all(tuple(small) + (full_last,))
    return results


def solution(mesh):
    in_specs = (P("dp", "ctx", None), P("dp", "ctx", None), P(), P(), P(), P(), P(), P())
    out_specs = (P(), P(), P(), P(), P())
    return jax.shard_map(
        on_device, mesh=mesh, in_specs=in_specs, out_specs=out_specs, check_vma=False
    )
```

```python
import functools
import math

import jax
import jax.numpy as jnp
import ml_dtypes
import numpy as np
from jax import lax
from jax.experimental import pallas as pl
from jax.experimental.pallas import tpu as pltpu
from jax.sharding import PartitionSpec as P

BANDS = 16
FB = 256
CC = 16
BF = jnp.bfloat16
F32 = jnp.float32
HI = lax.Precision.HIGHEST
MESH = pl.DeviceIdType.MESH


def make_tables(rows):
    seq = rows * FB
    half = rows + 1
    j = np.arange(half, dtype=np.int64)
    n = np.arange(rows, dtype=np.int64)
    m = np.arange(FB, dtype=np.int64)
    f32, bf = np.float32, ml_dtypes.bfloat16
    ang = (f32(math.pi) * (j[:, None] * n[None, :] % (2 * rows)).astype(f32) / f32(rows)).astype(f32)
    fr = np.cos(ang).astype(bf).astype(f32)
    fi = (-np.sin(ang)).astype(bf).astype(f32)
    ang = (f32(2.0 * math.pi) * (m[:, None] * m[None, :] % FB).astype(f32) / f32(FB)).astype(f32)
    er = np.cos(ang).astype(bf).astype(f32)
    ei = (-np.sin(ang)).astype(bf).astype(f32)
    ang = (f32(math.pi) * (j[:, None] * m[None, :] % (2 * seq)).astype(f32) / f32(seq)).astype(f32)
    tw = np.stack([np.cos(ang), -np.sin(ang)]).astype(f32)
    eye = np.eye(CC, dtype=f32)
    forward = np.kron(np.concatenate([fr, fi], 0), eye).astype(bf)
    e_fwd = np.block([[er.T, ei.T], [-ei.T, er.T]]).astype(bf)
    e_inv = np.block([[er.T, -ei.T], [ei.T, er.T]]).astype(bf)
    twice = np.where(j % rows == 0, 1.0, 2.0).astype(f32)[:, None]
    both = np.concatenate([fr * twice, (fi * twice)[1:rows]], 0) * f32(0.5 / seq)
    inverse = np.kron(both.T, eye).astype(bf)
    q = np.arange(seq, dtype=np.int64)
    band = np.arange(1, BANDS + 1, dtype=np.int64)[:, None]
    ang = (f32(2.0 * math.pi) * (band * q[None, :] % seq).astype(f32) / f32(seq)).astype(f32)
    ramp = (q[None, :].astype(f32) / f32(seq)).astype(f32)
    feats = np.concatenate([ramp, np.cos(ang), np.sin(ang)], 0).astype(f32)
    return forward, e_fwd, e_inv, inverse, tw, feats


def nt(left, right):
    return lax.dot_general(left, right, (((1,), (1,)), ((), ())), preferred_element_type=F32)


def mm(left, right):
    return jnp.dot(left, right, preferred_element_type=F32)


def exact(left, right):
    return jnp.dot(left, right, precision=HI, preferred_element_type=F32)


def transform_kernel(
    parts,
    x_ref, g_ref, fwd_ref, ef_ref, ei_ref, inv_ref, tw_ref, feats_ref,
    wf_ref, bf_ref, wm_ref, wmt_ref, bm_ref, wl_ref, rate_ref,
    out_ref,
    send, recv, spec, back, act_x, cos_first, act_second, cos_second, feat_x, modul, shaped,
    send_sem, recv_sem,
):
    me = lax.axis_index("ctx")
    channels = x_ref.shape[1]
    own = channels // parts
    chunks = own // CC
    half = parts + 1
    order = feats_ref.shape[0]
    seq = feats_ref.shape[1]
    hidden = wm_ref.shape[0]

    barrier = pltpu.get_barrier_semaphore()

    @pl.loop(1, parts)
    def _(r):
        pl.semaphore_signal(
            barrier, inc=1, device_id={"ctx": lax.rem(me + r, parts)}, device_id_type=MESH
        )

    @pl.loop(0, channels // 128)
    def _(e):
        lanes = pl.ds(pl.multiple_of(e * 128, 128), 128)
        for v, ref in enumerate((x_ref, g_ref)):
            turned = ref[:, lanes].T
            for i in range(128 // own):
                for k in range(chunks):
                    row = i * own + k * CC
                    send[e * (128 // own) + i, k, v] = turned[row : row + CC]

    pl.semaphore_wait(barrier, parts - 1)
    mine = pl.ds(pl.multiple_of(me * CC, CC), CC)

    def copy_to(r, k):
        target = lax.rem(me + r, parts)
        return pltpu.make_async_remote_copy(
            src_ref=send.at[target, k],
            dst_ref=recv.at[k, :, mine],
            send_sem=send_sem.at[k],
            recv_sem=recv_sem.at[k],
            device_id={"ctx": target},
            device_id_type=MESH,
        )

    for k in range(chunks):

        @pl.loop(0, parts - 1)
        def _(i):
            step = i // 2 + 1
            r = jnp.where(lax.rem(i, 2) == 0, step, parts - step)
            copy_to(r, k).start()

    for k in range(chunks):
        recv[k, :, mine] = send[me, k]

    width = 512
    act_x[hidden:, :] = jnp.where(
        lax.broadcasted_iota(jnp.int32, (128 - hidden, seq), 0) == 34, 1.0, 0.0
    ).astype(BF)

    @pl.loop(0, seq // width)
    def _(i):
        at = pl.ds(pl.multiple_of(i * width, width), width)
        feats = feats_ref[:, at]
        pre_first = exact(wf_ref[...], feats) + bf_ref[...]
        first = jnp.sin(pre_first)
        cos_first[:, at] = jnp.cos(pre_first)
        act_x[:hidden, at] = first.astype(BF)
        pre_second = exact(wm_ref[...], first) + bm_ref[...]
        act_second[:, at] = jnp.sin(pre_second).astype(BF)
        cos_second[:, at] = jnp.cos(pre_second)
        places = (i * width + lax.broadcasted_iota(jnp.int32, (1, width), 1)).astype(F32)
        modul[:, at] = jnp.exp(-(rate_ref[...] * places) / seq)
        feat_x[:hidden, at] = jnp.zeros((hidden, width), BF)
        tail = jnp.concatenate(
            [feats, jnp.ones((1, width), F32), jnp.zeros((128 - hidden - order - 1, width), F32)], axis=0
        )
        feat_x[hidden:, at] = tail.astype(BF)

    @pl.loop(0, chunks)
    def _(k):
        for which in (send_sem, recv_sem):
            pltpu.make_async_copy(
                recv.at[k, :, : (parts - 1) * CC], recv.at[k, :, : (parts - 1) * CC], which.at[k]
            ).wait()
        turn_re = tw_ref[0][:, None, :]
        turn_im = tw_ref[1][:, None, :]
        for v in range(2):
            part = mm(fwd_ref[...], recv[k, v])
            part_re = part[: half * CC].reshape(half, CC, FB)
            part_im = part[half * CC :].reshape(half, CC, FB)
            spec[:, v, :, :FB] = (part_re * turn_re - part_im * turn_im).astype(BF)
            spec[:, v, :, FB:] = (part_re * turn_im + part_im * turn_re).astype(BF)
        both = mm(spec[...].reshape(half * 2 * CC, 2 * FB), ef_ref[...]).reshape(half, 2, CC, 2 * FB)
        x_re, x_im = both[:, 0, :, :FB], both[:, 0, :, FB:]
        g_re, g_im = both[:, 1, :, :FB], both[:, 1, :, FB:]
        cross = jnp.concatenate(
            [(x_re * g_re + x_im * g_im).astype(BF), (x_re * g_im - x_im * g_re).astype(BF)], axis=-1
        )
        inner = mm(cross.reshape(half * CC, 2 * FB), ei_ref[...]).reshape(half, CC, 2 * FB)
        in_re, in_im = inner[:, :, :FB], inner[:, :, FB:]
        back[:half] = (in_re * turn_re + in_im * turn_im).astype(BF)
        back[half:] = (in_im * turn_re - in_re * turn_im)[1:parts].astype(BF)
        grad = mm(inv_ref[...], back[...].reshape(2 * parts * CC, FB))
        rows = pl.ds(pl.multiple_of(k * CC, CC), CC)
        for s in range(parts):
            at = slice(s * FB, (s + 1) * FB)
            shaped[rows, at] = (grad[s * CC : (s + 1) * CC] * modul[rows, at]).astype(BF)

    span = 1024
    wl = wl_ref[...].astype(BF)
    wmt = wmt_ref[...].astype(BF)

    def step(i, carry):
        last, small = carry
        at = pl.ds(pl.multiple_of(i * span, span), span)
        sh = shaped[:, at]
        last = last + nt(act_second[:, at], sh)
        d_second = (mm(wl, sh) * cos_second[:, at]).astype(BF)
        d_first = (mm(wmt, d_second) * cos_first[:, at]).astype(BF)
        small = small + nt(d_second, act_x[:, at]) + nt(d_first, feat_x[:, at])
        return last, small

    last, small = lax.fori_loop(
        0, seq // span, step, (jnp.zeros((hidden, own), F32), jnp.zeros((hidden, 128), F32))
    )
    last = jnp.concatenate([last, jnp.zeros((hidden, 128 - own), F32)], axis=1)
    odd = lax.rem(me, 2) == 1
    last = jnp.where(odd, pltpu.roll(last, own, 1), last)
    groups = out_ref.shape[0]
    out_ref[:, : hidden // groups] = last.reshape(groups, hidden // groups, 128)
    out_ref[:, hidden // groups :] = small.reshape(groups, hidden // groups, 128)


def reduce_kernel(
    groups, parts, count,
    part_ref,
    last_ref, mid_ref, turned_ref, factor_ref,
    got, own, ring, fin, small,
    sems,
):
    dp = lax.axis_index("dp")
    ctx = lax.axis_index("ctx")
    rows = part_ref.shape[1] // 2

    barrier = pltpu.get_barrier_semaphore()

    @pl.loop(1, parts)
    def _(r):
        pl.semaphore_signal(
            barrier, inc=1, device_id={"ctx": lax.rem(ctx + r, parts)}, device_id_type=MESH
        )

    @pl.loop(1, groups)
    def _(r):
        pl.semaphore_signal(
            barrier, inc=1, device_id={"dp": lax.rem(dp + r, groups)}, device_id_type=MESH
        )

    pl.semaphore_wait(barrier, parts + groups - 2)

    def wait(ref, send, recv):
        for which in (send, recv):
            pltpu.make_async_copy(ref, ref, sems.at[which]).wait()

    @pl.loop(1, groups)
    def _(r):
        target = lax.rem(dp + r, groups)
        pltpu.make_async_remote_copy(
            src_ref=part_ref.at[target], dst_ref=got.at[groups - r],
            send_sem=sems.at[0], recv_sem=sems.at[1],
            device_id={"dp": target}, device_id_type=MESH,
        ).start()

    wait(got.at[1:groups], 0, 1)
    total = part_ref[dp]
    for r in range(1, groups):
        total = total + got[r]
    own[...] = total
    ring[0] = total

    @pl.loop(1, parts)
    def _(r):
        target = lax.rem(ctx + r, parts)
        pltpu.make_async_remote_copy(
            src_ref=own, dst_ref=ring.at[parts - r],
            send_sem=sems.at[2], recv_sem=sems.at[3],
            device_id={"ctx": target}, device_id_type=MESH,
        ).start()

    wait(ring.at[1:parts], 2, 3)
    low = lax.broadcasted_iota(jnp.int32, (rows, 128), 1) < 64
    summed = jnp.zeros((rows, 128), F32)
    for e in range(parts // 2):
        first = ring[lax.rem(2 * e + parts - ctx, parts)]
        second = ring[lax.rem(2 * e + 1 + parts - ctx, parts)]
        fin[dp, :, 128 * e : 128 * (e + 1)] = jnp.where(low, first[:rows], second[:rows]).astype(BF)
        summed = summed + first[rows:] + second[rows:]
    small[dp] = summed

    @pl.loop(1, groups)
    def _(r):
        target = lax.rem(dp + r, groups)
        for ref, base in ((fin, 4), (small, 6)):
            pltpu.make_async_remote_copy(
                src_ref=ref.at[dp], dst_ref=ref.at[dp],
                send_sem=sems.at[base], recv_sem=sems.at[base + 1],
                device_id={"dp": target}, device_id_type=MESH,
            ).start()

    wait(fin.at[: groups - 1], 4, 5)
    wait(small.at[: groups - 1], 6, 7)
    grads = fin[...].astype(F32)
    others = small[...].reshape(groups * rows, 128)
    squares = jnp.sum(jnp.sum(grads * grads, axis=0), keepdims=True) + jnp.sum(others * others, keepdims=True)
    factor = jnp.minimum(1.0, math.sqrt(count) / (jnp.sqrt(squares) + 1e-06))
    last_ref[...] = fin[...]
    mid_ref[...] = others * factor
    turned_ref[...] = (others * factor).T
    factor_ref[...] = jnp.broadcast_to(factor, (8, 128))


def on_device(inputs, grad_out, w_first, b_first, w_mid, b_mid, w_last, decay_rate):
    parts = lax.axis_size("ctx")
    groups = lax.axis_size("dp")
    index = lax.axis_index("ctx")
    channels = inputs.shape[2]
    hidden, order = w_first.shape
    own = channels // parts
    chunks = own // CC
    half = parts + 1
    seq = parts * FB
    tables = make_tables(parts)
    w_own = lax.dynamic_slice_in_dim(w_last.T, index * own, own, 1)
    rates = lax.dynamic_slice_in_dim(decay_rate, index * own, own, 0)
    vmem = pl.BlockSpec(memory_space=pltpu.VMEM)
    part = pl.pallas_call(
        functools.partial(transform_kernel, parts),
        out_shape=jax.ShapeDtypeStruct((groups, 2 * hidden // groups, 128), F32),
        in_specs=[vmem] * 15,
        out_specs=vmem,
        scratch_shapes=[
            pltpu.VMEM((parts, chunks, 2, CC, FB), BF),
            pltpu.VMEM((chunks, 2, parts * CC, FB), BF),
            pltpu.VMEM((half, 2, CC, 2 * FB), BF),
            pltpu.VMEM((2 * parts, CC, FB), BF),
            pltpu.VMEM((128, seq), BF),
            pltpu.VMEM((hidden, seq), F32),
            pltpu.VMEM((hidden, seq), BF),
            pltpu.VMEM((hidden, seq), F32),
            pltpu.VMEM((128, seq), BF),
            pltpu.VMEM((own, seq), F32),
            pltpu.VMEM((own, seq), BF),
            pltpu.SemaphoreType.DMA((chunks,)),
            pltpu.SemaphoreType.DMA((chunks,)),
        ],
        compiler_params=pltpu.CompilerParams(
            collective_id=0, has_side_effects=True, vmem_limit_bytes=60 * 1024 * 1024
        ),
    )(
        inputs[0], grad_out[0], *tables,
        w_first, b_first[:, None], w_mid, w_mid.T, b_mid[:, None], w_own, rates[:, None],
    )
    count = hidden * (order + hidden + 2) + channels * hidden
    last, mid, turned, factor = pl.pallas_call(
        functools.partial(reduce_kernel, groups, parts, count),
        out_shape=(
            jax.ShapeDtypeStruct((groups, hidden // groups, channels), BF),
            jax.ShapeDtypeStruct((hidden, 128), F32),
            jax.ShapeDtypeStruct((128, hidden), F32),
            jax.ShapeDtypeStruct((8, 128), F32),
        ),
        in_specs=[vmem],
        out_specs=(vmem,) * 4,
        scratch_shapes=[
            pltpu.VMEM((groups, 2 * hidden // groups, 128), F32),
            pltpu.VMEM((2 * hidden // groups, 128), F32),
            pltpu.VMEM((parts, 2 * hidden // groups, 128), F32),
            pltpu.VMEM((groups, hidden // groups, channels), BF),
            pltpu.VMEM((groups, hidden // groups, 128), F32),
            pltpu.SemaphoreType.DMA((8,)),
        ],
        compiler_params=pltpu.CompilerParams(
            collective_id=1, has_side_effects=True, vmem_limit_bytes=32 * 1024 * 1024
        ),
    )(part)
    clip_last = (last.reshape(hidden, channels).astype(F32) * factor[0, 0]).T
    clip_first = turned[hidden : hidden + order].T
    return (clip_first, turned[hidden + order], mid[:, :hidden], turned[hidden + order + 1], clip_last)


def solution(mesh):
    in_specs = (P("dp", "ctx", None), P("dp", "ctx", None), P(), P(), P(), P(), P(), P())
    out_specs = (P(), P(), P(), P(), P())
    return jax.shard_map(
        on_device, mesh=mesh, in_specs=in_specs, out_specs=out_specs, check_vma=False
    )
```

```python
import functools
import math

import jax
import jax.numpy as jnp
import ml_dtypes
import numpy as np
from jax import lax
from jax.experimental import pallas as pl
from jax.experimental.pallas import tpu as pltpu
from jax.sharding import PartitionSpec as P

BANDS = 16
FB = 256
CC = 16
BF = jnp.bfloat16
F32 = jnp.float32
MESH = pl.DeviceIdType.MESH
FP = 48
SPAN = 2048
PI_HIGH = 1.570770263671875
PI_LOW = math.pi / 2 - PI_HIGH


def make_tables(rows):
    seq = rows * FB
    half = rows + 1
    j = np.arange(half, dtype=np.int64)
    n = np.arange(rows, dtype=np.int64)
    m = np.arange(FB, dtype=np.int64)
    f32, bf = np.float32, ml_dtypes.bfloat16
    ang = (f32(math.pi) * (j[:, None] * n[None, :] % (2 * rows)).astype(f32) / f32(rows)).astype(f32)
    fr = np.cos(ang).astype(bf).astype(f32)
    fi = (-np.sin(ang)).astype(bf).astype(f32)
    ang = (f32(2.0 * math.pi) * (m[:, None] * m[None, :] % FB).astype(f32) / f32(FB)).astype(f32)
    er = np.cos(ang).astype(bf).astype(f32)
    ei = (-np.sin(ang)).astype(bf).astype(f32)
    ang = (f32(math.pi) * (j[:, None] * m[None, :] % (2 * seq)).astype(f32) / f32(seq)).astype(f32)
    tw = np.stack([np.cos(ang), -np.sin(ang)]).astype(f32)
    eye = np.eye(CC, dtype=f32)
    forward = np.kron(np.concatenate([fr, fi], 0), eye).astype(bf)
    e_fwd = np.block([[er.T, ei.T], [-ei.T, er.T]]).astype(bf)
    e_inv = np.block([[er.T, -ei.T], [ei.T, er.T]]).astype(bf)
    twice = np.where(j % rows == 0, 1.0, 2.0).astype(f32)[:, None]
    both = np.concatenate([fr * twice, (fi * twice)[1:rows]], 0) * f32(0.5 / seq)
    inverse = np.kron(both.T, eye).astype(bf)
    q = np.arange(seq, dtype=np.int64)
    band = np.arange(1, BANDS + 1, dtype=np.int64)[:, None]
    ang = (f32(2.0 * math.pi) * (band * q[None, :] % seq).astype(f32) / f32(seq)).astype(f32)
    ramp = (q[None, :].astype(f32) / f32(seq)).astype(f32)
    feats = np.concatenate([ramp, np.cos(ang), np.sin(ang)], 0).astype(f32)
    high = feats.astype(bf)
    low = (feats - high.astype(f32)).astype(bf)
    zero = np.zeros((FP - feats.shape[0], seq), bf)
    ones = zero.copy()
    ones[0] = 1
    stack = np.concatenate([high, ones, low, zero], 0)
    return forward, e_fwd, e_inv, inverse, tw, stack


def nt(left, right):
    return lax.dot_general(left, right, (((1,), (1,)), ((), ())), preferred_element_type=F32)


def mm(left, right):
    return jnp.dot(left, right, preferred_element_type=F32)


def halves(value):
    high = value.astype(BF).astype(F32)
    return high, value - high


def column(row):
    n = row.shape[1]
    on = lax.broadcasted_iota(jnp.int32, (n, n), 0) == lax.broadcasted_iota(jnp.int32, (n, n), 1)
    return jnp.sum(jnp.where(on, jnp.broadcast_to(row, (n, n)), 0.0), axis=1, keepdims=True)


def sin_cos(value):
    turns = jnp.floor(value * (2.0 / math.pi) + 0.5)
    rest = (value - turns * PI_HIGH) - turns * PI_LOW
    square = rest * rest
    sine = rest + rest * square * (
        -1.6666654611e-1 + square * (8.3321608736e-3 + square * -1.9515295891e-4)
    )
    cosine = (1.0 - 0.5 * square) + square * square * (
        4.166664568298827e-2 + square * (-1.388731625493765e-3 + square * 2.443315711809948e-5)
    )
    quarter = turns.astype(jnp.int32)
    swap = (quarter & 1) == 1
    first = jnp.where(swap, cosine, sine)
    second = jnp.where(swap, sine, cosine)
    return (
        jnp.where((quarter & 2) == 2, -first, first),
        jnp.where(((quarter + 1) & 2) == 2, -second, second),
    )


def main_kernel(
    parts, groups,
    x_any, g_any, fwd_any, ef_any, ei_any, inv_any, tw_any, feats_any, wl_any,
    wf_ref, bf_ref, wm_ref, bm_ref, rate_ref,
    last_ref, small_ref,
    x_ref, g_ref, fwd_ref, ef_ref, ei_ref, inv_ref, tw_ref, feats_ref, wl_ref,
    send, recv, spec, back, cos_first, act_second, cos_second, wide, modul,
    part, got, own_part, ring, fin, small,
    load_sem, send_sem, recv_sem, sems,
):
    ctx = lax.axis_index("ctx")
    dp = lax.axis_index("dp")
    channels = x_ref.shape[1]
    own = channels // parts
    chunks = own // CC
    half = parts + 1
    order, hidden = wf_ref.shape
    seq = cos_first.shape[1]
    pair = 128 // own

    lanes_own = pl.ds(pl.multiple_of((ctx // pair) * 128, 128), 128)
    loads = [
        pltpu.make_async_copy(source, target, load_sem.at[i])
        for i, (source, target) in enumerate(
            (
                (x_any, x_ref), (g_any, g_ref), (wl_any.at[:, lanes_own], wl_ref), (feats_any, feats_ref),
                (tw_any, tw_ref), (fwd_any, fwd_ref), (ef_any, ef_ref), (ei_any, ei_ref), (inv_any, inv_ref),
            )
        )
    ]
    for load in loads:
        load.start()

    barrier = pltpu.get_barrier_semaphore()

    @pl.loop(1, parts)
    def _(r):
        pl.semaphore_signal(
            barrier, inc=1, device_id={"ctx": lax.rem(ctx + r, parts)}, device_id_type=MESH
        )

    @pl.loop(1, groups)
    def _(r):
        pl.semaphore_signal(
            barrier, inc=1, device_id={"dp": lax.rem(dp + r, groups)}, device_id_type=MESH
        )

    mine = pl.ds(pl.multiple_of(ctx * CC, CC), CC)

    def copy_to(target, k):
        return pltpu.make_async_remote_copy(
            src_ref=send.at[target, k],
            dst_ref=recv.at[k, :, mine],
            send_sem=send_sem.at[k],
            recv_sem=recv_sem.at[k],
            device_id={"ctx": target},
            device_id_type=MESH,
        )

    loads[0].wait()
    loads[1].wait()
    pl.semaphore_wait(barrier, parts + groups - 2)

    @pl.loop(0, channels // 128)
    def _(i):
        e = lax.rem(ctx // pair + i + 1, channels // 128)
        lanes = pl.ds(pl.multiple_of(e * 128, 128), 128)
        for v, ref in enumerate((x_ref, g_ref)):
            turned = ref[:, lanes].T
            for a in range(pair):
                for k in range(chunks):
                    row = a * own + k * CC
                    send[e * pair + a, k, v] = turned[row : row + CC]
        for a in range(pair):

            @pl.when(e * pair + a != ctx)
            def _():
                copy_to(e * pair + a, 0).start()

    for k in range(1, chunks):

        @pl.loop(0, parts - 1)
        def _(i):
            step = i // 2 + 1
            r = jnp.where(lax.rem(i, 2) == 0, step, parts - step)
            copy_to(lax.rem(ctx + r, parts), k).start()

    for k in range(chunks):
        recv[k, :, mine] = send[ctx, k]

    for load in loads[2:]:
        load.wait()
    width = 512
    top = 256 - own
    wf = jnp.concatenate([wf_ref[...], jnp.zeros((FP - order, hidden), F32)], axis=0)
    wf_high, wf_low = halves(wf)
    wf_stack = jnp.concatenate([wf_high, wf_high, wf_low], axis=0).T.astype(BF)
    wm_high, wm_low = halves(wm_ref[...])
    wm_stack = jnp.concatenate([wm_high.T, wm_high.T, wm_low.T], axis=0).T.astype(BF)
    first_bias = column(bf_ref[...].reshape(1, hidden))
    second_bias = column(bm_ref[...].reshape(1, hidden))
    odd = lax.rem(ctx, pair) == 1
    rates = rate_ref[lanes_own].reshape(1, 128)
    rates = jnp.where(odd, pltpu.roll(jnp.broadcast_to(rates, (8, 128)), own, 1)[:1], rates)
    decay = column(rates[:, :own])
    wide[hidden : hidden + FP] = feats_ref[:FP]
    wide[hidden + FP : 128] = jnp.zeros((128 - hidden - FP, seq), BF)
    wide[128 : 128 + FP] = feats_ref[FP:]
    wide[128 + FP : top] = jnp.zeros((top - 128 - FP, seq), BF)

    @pl.loop(0, seq // width)
    def _(i):
        at = pl.ds(pl.multiple_of(i * width, width), width)
        high = feats_ref[:FP, at]
        stack = jnp.concatenate([high, feats_ref[FP:, at], high], axis=0)
        first, cos_one = sin_cos(mm(wf_stack, stack) + first_bias)
        cos_first[:, at] = cos_one
        high, low = halves(first)
        high, low = high.astype(BF), low.astype(BF)
        wide[:hidden, at] = high
        stack = jnp.concatenate([high, low, high], axis=0)
        second, cos_two = sin_cos(mm(wm_stack, stack) + second_bias)
        act_second[:, at] = second.astype(BF)
        cos_second[:, at] = cos_two
        places = (i * width + lax.broadcasted_iota(jnp.int32, (1, width), 1)).astype(F32)
        modul[:, at] = jnp.exp(-(decay * places) / seq)

    @pl.loop(0, chunks)
    def _(k):
        for which in (send_sem, recv_sem):
            pltpu.make_async_copy(
                recv.at[k, :, : (parts - 1) * CC], recv.at[k, :, : (parts - 1) * CC], which.at[k]
            ).wait()
        turn_re = tw_ref[0][:, None, :]
        turn_im = tw_ref[1][:, None, :]
        for v in range(2):
            part_all = mm(fwd_ref[...], recv[k, v])
            part_re = part_all[: half * CC].reshape(half, CC, FB)
            part_im = part_all[half * CC :].reshape(half, CC, FB)
            spec[:, v, :, :FB] = (part_re * turn_re - part_im * turn_im).astype(BF)
            spec[:, v, :, FB:] = (part_re * turn_im + part_im * turn_re).astype(BF)
        both = mm(spec[...].reshape(half * 2 * CC, 2 * FB), ef_ref[...]).reshape(half, 2, CC, 2 * FB)
        x_re, x_im = both[:, 0, :, :FB], both[:, 0, :, FB:]
        g_re, g_im = both[:, 1, :, :FB], both[:, 1, :, FB:]
        cross = jnp.concatenate(
            [(x_re * g_re + x_im * g_im).astype(BF), (x_re * g_im - x_im * g_re).astype(BF)], axis=-1
        )
        inner = mm(cross.reshape(half * CC, 2 * FB), ei_ref[...]).reshape(half, CC, 2 * FB)
        in_re, in_im = inner[:, :, :FB], inner[:, :, FB:]
        back[:half] = (in_re * turn_re + in_im * turn_im).astype(BF)
        back[half:] = (in_im * turn_re - in_re * turn_im)[1:parts].astype(BF)
        grad = mm(inv_ref[...], back[...].reshape(2 * parts * CC, FB))
        first_row = pl.multiple_of(k * CC, CC)
        for s in range(parts):
            at = slice(s * FB, (s + 1) * FB)
            wide[pl.ds(top + first_row, CC), at] = (
                grad[s * CC : (s + 1) * CC] * modul[pl.ds(first_row, CC), at]
            ).astype(BF)

    span = SPAN
    tile = jnp.where(odd, pltpu.roll(wl_ref[...], own, 1), wl_ref[...])[:, :own]
    high, low = halves(tile.T)
    wl_stack = jnp.concatenate([high, low], axis=0).T.astype(BF)
    wmt_stack = jnp.concatenate([wm_high, wm_low], axis=0).T.astype(BF)
    total = jnp.zeros((3 * hidden, 256), F32)
    for i in range(seq // span):
        at = slice(i * span, (i + 1) * span)
        sh = wide[top:, at]
        d_second = (mm(wl_stack, jnp.concatenate([sh, sh], axis=0)) * cos_second[:, at]).astype(BF)
        d_first = (
            mm(wmt_stack, jnp.concatenate([d_second, d_second], axis=0)) * cos_first[:, at]
        ).astype(BF)
        lines = jnp.concatenate([d_second, d_first, act_second[:, at]], axis=0)
        total = total + nt(lines, wide[:, at])

    rows = hidden // groups
    lane = lax.broadcasted_iota(jnp.int32, (hidden, 128), 1)
    by_second, by_first = total[:hidden], total[hidden : 2 * hidden]
    at_bias = hidden + order
    mixed = by_first[:, :128] + pltpu.roll(by_first[:, 128:], hidden, 1)
    mixed = jnp.where(lane < hidden, by_second[:, :128], mixed)
    mixed = jnp.where(lane == at_bias + 1, pltpu.roll(by_second[:, :128], 1, 1), mixed)
    mixed = jnp.where(lane > at_bias + 1, 0.0, mixed)
    last = total[2 * hidden :, 128:]
    last = jnp.where(odd, last, pltpu.roll(last, own, 1))
    part[:, :rows] = last.reshape(groups, rows, 128)
    part[:, rows:] = mixed.reshape(groups, rows, 128)

    def wait(ref, first, second):
        for which in (first, second):
            pltpu.make_async_copy(ref, ref, sems.at[which]).wait()

    @pl.loop(1, groups)
    def _(r):
        target = lax.rem(dp + r, groups)
        pltpu.make_async_remote_copy(
            src_ref=part.at[target], dst_ref=got.at[groups - r],
            send_sem=sems.at[0], recv_sem=sems.at[1],
            device_id={"dp": target}, device_id_type=MESH,
        ).start()

    wait(got.at[1:groups], 0, 1)
    summed = part[dp]
    for r in range(1, groups):
        summed = summed + got[r]
    own_part[...] = summed
    ring[0] = summed

    @pl.loop(1, parts)
    def _(r):
        target = lax.rem(ctx + r, parts)
        pltpu.make_async_remote_copy(
            src_ref=own_part, dst_ref=ring.at[parts - r],
            send_sem=sems.at[2], recv_sem=sems.at[3],
            device_id={"ctx": target}, device_id_type=MESH,
        ).start()

    wait(ring.at[1:parts], 2, 3)
    low_lanes = lax.broadcasted_iota(jnp.int32, (rows, 128), 1) < own
    summed = jnp.zeros((rows, 128), F32)
    for e in range(parts // 2):
        one = ring[lax.rem(2 * e + parts - ctx, parts)]
        two = ring[lax.rem(2 * e + 1 + parts - ctx, parts)]
        fin[dp, :, 128 * e : 128 * (e + 1)] = jnp.where(low_lanes, one[:rows], two[:rows]).astype(BF)
        summed = summed + one[rows:] + two[rows:]
    small[dp] = summed

    @pl.loop(1, groups)
    def _(r):
        target = lax.rem(dp + r, groups)
        for ref, base in ((fin, 4), (small, 6)):
            pltpu.make_async_remote_copy(
                src_ref=ref.at[dp], dst_ref=ref.at[dp],
                send_sem=sems.at[base], recv_sem=sems.at[base + 1],
                device_id={"dp": target}, device_id_type=MESH,
            ).start()

    wait(fin.at[: groups - 1], 4, 5)
    wait(small.at[: groups - 1], 6, 7)
    last_ref[...] = fin[...]
    small_ref[...] = small[...]


def clip_kernel(count, last_in, small_in, first_ref, first_bias_ref, mid_ref, mid_bias_ref, last_ref):
    groups, rows, channels = last_in.shape
    hidden = groups * rows
    order = first_ref.shape[0]
    grads = last_in[...].astype(F32)
    others = small_in[...].reshape(hidden, 128)
    squares = jnp.sum(jnp.sum(grads * grads, axis=0), keepdims=True) + jnp.sum(others * others, keepdims=True)
    factor = jnp.minimum(1.0, math.sqrt(count) / (jnp.sqrt(squares) + 1e-06))
    last_ref[...] = grads.reshape(hidden, channels) * factor
    others = others * factor
    mid_ref[...] = others[:, :hidden]
    turned = others.T
    first_ref[...] = turned[hidden : hidden + order]
    first_bias_ref[...] = turned[hidden + order]
    mid_bias_ref[...] = turned[hidden + order + 1]


def on_device(inputs, grad_out, w_first, b_first, w_mid, b_mid, w_last, decay_rate):
    parts = lax.axis_size("ctx")
    groups = lax.axis_size("dp")
    channels = inputs.shape[2]
    hidden, order = w_first.shape
    own = channels // parts
    chunks = own // CC
    half = parts + 1
    seq = parts * FB
    rows = hidden // groups
    tables = make_tables(parts)
    vmem = pl.BlockSpec(memory_space=pltpu.VMEM)
    anywhere = pl.BlockSpec(memory_space=pl.ANY)
    last, small = pl.pallas_call(
        functools.partial(main_kernel, parts, groups),
        out_shape=(
            jax.ShapeDtypeStruct((groups, rows, channels), BF),
            jax.ShapeDtypeStruct((groups, rows, 128), F32),
        ),
        in_specs=[anywhere] * 9 + [vmem] * 5,
        out_specs=(vmem, vmem),
        scratch_shapes=[
            pltpu.VMEM((FB, channels), BF),
            pltpu.VMEM((FB, channels), BF),
            *(pltpu.VMEM(table.shape, table.dtype) for table in tables),
            pltpu.VMEM((hidden, 128), F32),
            pltpu.VMEM((parts, chunks, 2, CC, FB), BF),
            pltpu.VMEM((chunks, 2, parts * CC, FB), BF),
            pltpu.VMEM((half, 2, CC, 2 * FB), BF),
            pltpu.VMEM((2 * parts, CC, FB), BF),
            pltpu.VMEM((hidden, seq), F32),
            pltpu.VMEM((hidden, seq), BF),
            pltpu.VMEM((hidden, seq), F32),
            pltpu.VMEM((256, seq), BF),
            pltpu.VMEM((own, seq), F32),
            pltpu.VMEM((groups, 2 * rows, 128), F32),
            pltpu.VMEM((groups, 2 * rows, 128), F32),
            pltpu.VMEM((2 * rows, 128), F32),
            pltpu.VMEM((parts, 2 * rows, 128), F32),
            pltpu.VMEM((groups, rows, channels), BF),
            pltpu.VMEM((groups, rows, 128), F32),
            pltpu.SemaphoreType.DMA((9,)),
            pltpu.SemaphoreType.DMA((chunks,)),
            pltpu.SemaphoreType.DMA((chunks,)),
            pltpu.SemaphoreType.DMA((8,)),
        ],
        compiler_params=pltpu.CompilerParams(
            collective_id=0, has_side_effects=True, vmem_limit_bytes=60 * 1024 * 1024
        ),
    )(
        inputs[0], grad_out[0], *tables, w_last.T,
        w_first.T, b_first, w_mid, b_mid, decay_rate,
    )
    count = hidden * (order + hidden + 2) + channels * hidden
    first, first_bias, mid, mid_bias, last = pl.pallas_call(
        functools.partial(clip_kernel, count),
        out_shape=(
            jax.ShapeDtypeStruct((order, hidden), F32),
            jax.ShapeDtypeStruct((hidden,), F32),
            jax.ShapeDtypeStruct((hidden, hidden), F32),
            jax.ShapeDtypeStruct((hidden,), F32),
            jax.ShapeDtypeStruct((hidden, channels), F32),
        ),
        in_specs=[vmem] * 2,
        out_specs=(vmem,) * 5,
    )(last, small)
    return (first.T, first_bias, mid, mid_bias, last.T)


def solution(mesh):
    in_specs = (P("dp", "ctx", None), P("dp", "ctx", None), P(), P(), P(), P(), P(), P())
    out_specs = (P(), P(), P(), P(), P())
    return jax.shard_map(
        on_device, mesh=mesh, in_specs=in_specs, out_specs=out_specs, check_vma=False
    )
```

```python
import functools
import math

import jax
import jax.numpy as jnp
import ml_dtypes
import numpy as np
from jax import lax
from jax.experimental import pallas as pl
from jax.experimental.pallas import tpu as pltpu
from jax.sharding import PartitionSpec as P

BANDS = 16
FB = 256
CC = 16
BF = jnp.bfloat16
F32 = jnp.float32
MESH = pl.DeviceIdType.MESH
FP = 48
SPAN = 2048
NX = 4
PI_HIGH = 1.570770263671875
PI_LOW = math.pi / 2 - PI_HIGH


def make_tables(rows):
    seq = rows * FB
    half = rows + 1
    j = np.arange(half, dtype=np.int64)
    n = np.arange(rows, dtype=np.int64)
    m = np.arange(FB, dtype=np.int64)
    f32, bf = np.float32, ml_dtypes.bfloat16
    ang = (f32(math.pi) * (j[:, None] * n[None, :] % (2 * rows)).astype(f32) / f32(rows)).astype(f32)
    fr = np.cos(ang).astype(bf).astype(f32)
    fi = (-np.sin(ang)).astype(bf).astype(f32)
    ang = (f32(2.0 * math.pi) * (m[:, None] * m[None, :] % FB).astype(f32) / f32(FB)).astype(f32)
    er = np.cos(ang).astype(bf).astype(f32)
    ei = (-np.sin(ang)).astype(bf).astype(f32)
    ang = (f32(math.pi) * (j[:, None] * m[None, :] % (2 * seq)).astype(f32) / f32(seq)).astype(f32)
    tw = np.stack([np.cos(ang), -np.sin(ang)]).astype(f32)
    eye = np.eye(CC, dtype=f32)
    by_x = n.reshape(rows // NX, NX).T.reshape(-1)
    forward = np.kron(np.concatenate([fr, fi], 0)[:, by_x], eye).astype(bf)
    e_fwd = np.block([[er.T, ei.T], [-ei.T, er.T]]).astype(bf)
    e_inv = np.block([[er.T, -ei.T], [ei.T, er.T]]).astype(bf)
    twice = np.where(j % rows == 0, 1.0, 2.0).astype(f32)[:, None]
    both = np.concatenate([fr * twice, (fi * twice)[1:rows]], 0) * f32(0.5 / seq)
    inverse = np.kron(both.T, eye).astype(bf)
    q = np.arange(seq, dtype=np.int64)
    band = np.arange(1, BANDS + 1, dtype=np.int64)[:, None]
    ang = (f32(2.0 * math.pi) * (band * q[None, :] % seq).astype(f32) / f32(seq)).astype(f32)
    ramp = (q[None, :].astype(f32) / f32(seq)).astype(f32)
    feats = np.concatenate([ramp, np.cos(ang), np.sin(ang)], 0).astype(f32)
    high = feats.astype(bf)
    low = (feats - high.astype(f32)).astype(bf)
    zero = np.zeros((FP - feats.shape[0], seq), bf)
    ones = zero.copy()
    ones[0] = 1
    stack = np.concatenate([high, ones, low, zero], 0)
    return forward, e_fwd, e_inv, inverse, tw, stack


def nt(left, right):
    return lax.dot_general(left, right, (((1,), (1,)), ((), ())), preferred_element_type=F32)


def mm(left, right):
    return jnp.dot(left, right, preferred_element_type=F32)


def halves(value):
    high = value.astype(BF).astype(F32)
    return high, value - high


def column(row):
    n = row.shape[1]
    on = lax.broadcasted_iota(jnp.int32, (n, n), 0) == lax.broadcasted_iota(jnp.int32, (n, n), 1)
    return jnp.sum(jnp.where(on, jnp.broadcast_to(row, (n, n)), 0.0), axis=1, keepdims=True)


def sin_cos(value):
    turns = jnp.floor(value * (2.0 / math.pi) + 0.5)
    rest = (value - turns * PI_HIGH) - turns * PI_LOW
    square = rest * rest
    sine = rest + rest * square * (
        -1.6666654611e-1 + square * (8.3321608736e-3 + square * -1.9515295891e-4)
    )
    cosine = (1.0 - 0.5 * square) + square * square * (
        4.166664568298827e-2 + square * (-1.388731625493765e-3 + square * 2.443315711809948e-5)
    )
    quarter = turns.astype(jnp.int32)
    swap = (quarter & 1) == 1
    first = jnp.where(swap, cosine, sine)
    second = jnp.where(swap, sine, cosine)
    return (
        jnp.where((quarter & 2) == 2, -first, first),
        jnp.where(((quarter + 1) & 2) == 2, -second, second),
    )


def ahead(place, step, count):
    there = place + step
    return jnp.where(there >= count, there - count, there)


def behind(place, step, count):
    there = place - step
    return jnp.where(there < 0, there + count, there)


def main_kernel(
    parts, groups,
    x_any, g_any, fwd_any, ef_any, ei_any, inv_any, tw_any, feats_any, wl_any,
    wf_ref, bf_ref, wm_ref, bm_ref, rate_ref,
    last_ref, small_ref,
    x_ref, g_ref, fwd_ref, ef_ref, ei_ref, inv_ref, tw_ref, feats_ref, wl_ref,
    send, relay, recv, spec, back, cos_first, act_second, cos_second, wide, modul,
    part, got, ring, column_last, column_small, fin, small,
    load_sem, send_sem, relay_sem, recv_sem, sems,
):
    ctx = lax.axis_index("ctx")
    dp = lax.axis_index("dp")
    channels = x_ref.shape[1]
    own = channels // parts
    chunks = own // CC
    half = parts + 1
    order, hidden = wf_ref.shape
    seq = cos_first.shape[1]
    pair = 128 // own

    lanes_own = pl.ds(pl.multiple_of((ctx // pair) * 128, 128), 128)
    loads = [
        pltpu.make_async_copy(source, target, load_sem.at[i])
        for i, (source, target) in enumerate(
            (
                (x_any, x_ref), (g_any, g_ref), (wl_any.at[:, lanes_own], wl_ref), (feats_any, feats_ref),
                (tw_any, tw_ref), (fwd_any, fwd_ref), (ef_any, ef_ref), (ei_any, ei_ref), (inv_any, inv_ref),
            )
        )
    ]
    for load in loads:
        load.start()

    nz = parts // NX
    z, x = ctx // NX, lax.rem(ctx, NX)
    round_x = [ahead(x, r, NX) for r in range(NX)]
    round_z = [ahead(z, r, nz) for r in range(nz)]
    round_dp = [ahead(dp, r, groups) for r in range(groups)]
    peers_x = [{"ctx": z * NX + t} for t in round_x]
    peers_z = [{"ctx": t * NX + x} for t in round_z]
    peers_dp = [{"dp": t} for t in round_dp]

    barrier = pltpu.get_barrier_semaphore()
    for peer in peers_z[1:] + peers_x[1:] + peers_dp[1:]:
        pl.semaphore_signal(barrier, inc=1, device_id=peer, device_id_type=MESH)

    loads[0].wait()
    loads[1].wait()

    @pl.loop(0, channels // 128)
    def _(e):
        lanes = pl.ds(pl.multiple_of(e * 128, 128), 128)
        for v, ref in enumerate((x_ref, g_ref)):
            turned = ref[:, lanes].T
            for a in range(pair):
                to_z = (e * pair) // NX
                to_x = lax.rem(e * pair, NX) + a
                for k in range(chunks):
                    row = a * own + k * CC
                    send[to_z, to_x, k, v] = turned[row : row + CC]

    pl.semaphore_wait(barrier, nz + NX + groups - 3)

    def start(source, target, first, second, peer):
        pltpu.make_async_remote_copy(
            src_ref=source, dst_ref=target, send_sem=first, recv_sem=second,
            device_id=peer, device_id_type=MESH,
        ).start()

    for k in range(chunks):
        for r in range(1, NX):
            start(
                send.at[:, round_x[r], k], relay.at[k, :, :, NX - r], send_sem.at[k], relay_sem.at[k], peers_x[r]
            )
        for r in range(1, nz):
            start(
                send.at[round_z[r], x, k], recv.at[k, :, z, 0], send_sem.at[chunks + k], recv_sem.at[k], peers_z[r]
            )

    for k in range(chunks):
        recv[k, :, z, 0] = send[z, x, k]

    def forward(k):
        landed = relay.at[k, :, :, 1:]
        pltpu.make_async_copy(landed, landed, relay_sem.at[k]).wait()
        for r in range(1, nz):
            start(
                relay.at[k, round_z[r], :, 1:], recv.at[k, :, z, 1:], send_sem.at[2 * chunks + k], recv_sem.at[k],
                peers_z[r],
            )
        recv[k, :, z, 1:] = relay[k, z, :, 1:]

    for load in loads[2:]:
        load.wait()
    width = 512
    top = 256 - own
    wf = jnp.concatenate([wf_ref[...], jnp.zeros((FP - order, hidden), F32)], axis=0)
    wf_high, wf_low = halves(wf)
    wf_stack = jnp.concatenate([wf_high, wf_high, wf_low], axis=0).T.astype(BF)
    wm_high, wm_low = halves(wm_ref[...])
    wm_stack = jnp.concatenate([wm_high.T, wm_high.T, wm_low.T], axis=0).T.astype(BF)
    first_bias = column(bf_ref[...].reshape(1, hidden))
    second_bias = column(bm_ref[...].reshape(1, hidden))
    odd = lax.rem(ctx, pair) == 1
    rates = rate_ref[lanes_own].reshape(1, 128)
    rates = jnp.where(odd, pltpu.roll(jnp.broadcast_to(rates, (8, 128)), own, 1)[:1], rates)
    decay = column(rates[:, :own])
    wide[hidden : hidden + FP] = feats_ref[:FP]
    wide[hidden + FP : 128] = jnp.zeros((128 - hidden - FP, seq), BF)
    wide[128 : 128 + FP] = feats_ref[FP:]
    wide[128 + FP : top] = jnp.zeros((top - 128 - FP, seq), BF)

    def network(i):
        at = pl.ds(pl.multiple_of(i * width, width), width)
        high = feats_ref[:FP, at]
        stack = jnp.concatenate([high, feats_ref[FP:, at], high], axis=0)
        first, cos_one = sin_cos(mm(wf_stack, stack) + first_bias)
        cos_first[:, at] = cos_one
        high, low = halves(first)
        high, low = high.astype(BF), low.astype(BF)
        wide[:hidden, at] = high
        stack = jnp.concatenate([high, low, high], axis=0)
        second, cos_two = sin_cos(mm(wm_stack, stack) + second_bias)
        act_second[:, at] = second.astype(BF)
        cos_second[:, at] = cos_two
        places = (i * width + lax.broadcasted_iota(jnp.int32, (1, width), 1)).astype(F32)
        modul[:, at] = jnp.exp(-(decay * places) / seq)

    steps = seq // width
    pl.loop(0, steps * 3 // 4)(network)
    forward(0)
    pl.loop(steps * 3 // 4, steps)(network)
    for k in range(1, chunks):
        forward(k)

    @pl.loop(0, chunks)
    def _(k):
        landed = recv.at[k, :, : nz - 1]
        pltpu.make_async_copy(landed, landed, recv_sem.at[k]).wait()
        turn_re = tw_ref[0][:, None, :]
        turn_im = tw_ref[1][:, None, :]
        for v in range(2):
            columns = [
                recv[k, v, :, behind(t, x, NX)].reshape(nz * CC, FB) for t in range(NX)
            ]
            part_all = mm(fwd_ref[...], jnp.concatenate(columns, axis=0))
            part_re = part_all[: half * CC].reshape(half, CC, FB)
            part_im = part_all[half * CC :].reshape(half, CC, FB)
            spec[:, v, :, :FB] = (part_re * turn_re - part_im * turn_im).astype(BF)
            spec[:, v, :, FB:] = (part_re * turn_im + part_im * turn_re).astype(BF)
        both = mm(spec[...].reshape(half * 2 * CC, 2 * FB), ef_ref[...]).reshape(half, 2, CC, 2 * FB)
        x_re, x_im = both[:, 0, :, :FB], both[:, 0, :, FB:]
        g_re, g_im = both[:, 1, :, :FB], both[:, 1, :, FB:]
        cross = jnp.concatenate(
            [(x_re * g_re + x_im * g_im).astype(BF), (x_re * g_im - x_im * g_re).astype(BF)], axis=-1
        )
        inner = mm(cross.reshape(half * CC, 2 * FB), ei_ref[...]).reshape(half, CC, 2 * FB)
        in_re, in_im = inner[:, :, :FB], inner[:, :, FB:]
        back[:half] = (in_re * turn_re + in_im * turn_im).astype(BF)
        back[half:] = (in_im * turn_re - in_re * turn_im)[1:parts].astype(BF)
        grad = mm(inv_ref[...], back[...].reshape(2 * parts * CC, FB))
        first_row = pl.multiple_of(k * CC, CC)
        for s in range(parts):
            at = slice(s * FB, (s + 1) * FB)
            wide[pl.ds(top + first_row, CC), at] = (
                grad[s * CC : (s + 1) * CC] * modul[pl.ds(first_row, CC), at]
            ).astype(BF)

    span = SPAN
    tile = jnp.where(odd, pltpu.roll(wl_ref[...], own, 1), wl_ref[...])[:, :own]
    high, low = halves(tile.T)
    wl_stack = jnp.concatenate([high, low], axis=0).T.astype(BF)
    wmt_stack = jnp.concatenate([wm_high, wm_low], axis=0).T.astype(BF)
    total = jnp.zeros((3 * hidden, 256), F32)
    for i in range(seq // span):
        at = slice(i * span, (i + 1) * span)
        sh = wide[top:, at]
        d_second = (mm(wl_stack, jnp.concatenate([sh, sh], axis=0)) * cos_second[:, at]).astype(BF)
        d_first = (
            mm(wmt_stack, jnp.concatenate([d_second, d_second], axis=0)) * cos_first[:, at]
        ).astype(BF)
        lines = jnp.concatenate([d_second, d_first, act_second[:, at]], axis=0)
        total = total + nt(lines, wide[:, at])

    rows = hidden // groups
    lane = lax.broadcasted_iota(jnp.int32, (hidden, 128), 1)
    by_second, by_first = total[:hidden], total[hidden : 2 * hidden]
    at_bias = hidden + order
    mixed = by_first[:, :128] + pltpu.roll(by_first[:, 128:], hidden, 1)
    mixed = jnp.where(lane < hidden, by_second[:, :128], mixed)
    mixed = jnp.where(lane == at_bias + 1, pltpu.roll(by_second[:, :128], 1, 1), mixed)
    mixed = jnp.where(lane > at_bias + 1, 0.0, mixed)
    last = total[2 * hidden :, 128:]
    last = jnp.where(odd, last, pltpu.roll(last, own, 1))
    part[:, :rows] = last.reshape(groups, rows, 128)
    part[:, rows:] = mixed.reshape(groups, rows, 128)

    def wait(ref, which):
        pltpu.make_async_copy(ref, ref, sems.at[which]).wait()

    for r in range(1, groups):
        start(part.at[round_dp[r]], got.at[groups - r], sems.at[0], sems.at[1], peers_dp[r])
    wait(got.at[1:groups], 1)
    summed = part[dp]
    for r in range(1, groups):
        summed = summed + got[r]
    ring[0] = summed

    for r in range(1, nz):
        start(ring.at[0], ring.at[nz - r], sems.at[2], sems.at[3], peers_z[r])
    wait(ring.at[1:nz], 3)
    summed = jnp.zeros((rows, 128), F32)
    for t in range(nz):
        block = ring[behind(t, z, nz)]
        column_last[0, t] = block[:rows].astype(BF)
        summed = summed + block[rows:]
    column_small[0] = summed

    for r in range(1, NX):
        start(column_last.at[0], column_last.at[NX - r], sems.at[4], sems.at[5], peers_x[r])
        start(column_small.at[0], column_small.at[NX - r], sems.at[6], sems.at[7], peers_x[r])
    wait(column_last.at[1:NX], 5)
    wait(column_small.at[1:NX], 7)
    small[dp] = jnp.sum(column_small[...], axis=0)
    for t in range(0, NX, 2):
        one = column_last[behind(t, x, NX)].astype(F32)
        two = column_last[behind(t + 1, x, NX)].astype(F32)
        both = jnp.where(lax.broadcasted_iota(jnp.int32, one.shape, 2) < own, one, two).astype(BF)
        for i in range(nz):
            at = (i * NX + t) // 2 * 128
            fin[dp, :, at : at + 128] = both[i]

    for r in range(1, groups):
        start(fin.at[dp], fin.at[dp], sems.at[8], sems.at[9], peers_dp[r])
        start(small.at[dp], small.at[dp], sems.at[10], sems.at[11], peers_dp[r])
    wait(fin.at[: groups - 1], 9)
    wait(small.at[: groups - 1], 11)
    last_ref[...] = fin[...]
    small_ref[...] = small[...]

    wait(got.at[1:groups], 0)
    wait(ring.at[1:nz], 2)
    wait(column_last.at[1:NX], 4)
    wait(column_small.at[1:NX], 6)
    wait(fin.at[: groups - 1], 8)
    wait(small.at[: groups - 1], 10)
    for k in range(chunks):
        for i, ref in enumerate((relay.at[k, :, :, 1:], recv.at[k, :, : nz - 1, 0], recv.at[k, :, : nz - 1, 1:])):
            pltpu.make_async_copy(ref, ref, send_sem.at[i * chunks + k]).wait()


def clip_kernel(count, last_in, small_in, first_ref, first_bias_ref, mid_ref, mid_bias_ref, last_ref):
    groups, rows, channels = last_in.shape
    hidden = groups * rows
    order = first_ref.shape[0]
    grads = last_in[...].astype(F32)
    others = small_in[...].reshape(hidden, 128)
    squares = jnp.sum(jnp.sum(grads * grads, axis=0), keepdims=True) + jnp.sum(others * others, keepdims=True)
    factor = jnp.minimum(1.0, math.sqrt(count) / (jnp.sqrt(squares) + 1e-06))
    last_ref[...] = grads.reshape(hidden, channels) * factor
    others = others * factor
    mid_ref[...] = others[:, :hidden]
    turned = others.T
    first_ref[...] = turned[hidden : hidden + order]
    first_bias_ref[...] = turned[hidden + order]
    mid_bias_ref[...] = turned[hidden + order + 1]


def on_device(inputs, grad_out, w_first, b_first, w_mid, b_mid, w_last, decay_rate):
    parts = lax.axis_size("ctx")
    groups = lax.axis_size("dp")
    channels = inputs.shape[2]
    hidden, order = w_first.shape
    own = channels // parts
    chunks = own // CC
    half = parts + 1
    seq = parts * FB
    rows = hidden // groups
    nz = parts // NX
    tables = make_tables(parts)
    vmem = pl.BlockSpec(memory_space=pltpu.VMEM)
    anywhere = pl.BlockSpec(memory_space=pl.ANY)
    last, small = pl.pallas_call(
        functools.partial(main_kernel, parts, groups),
        out_shape=(
            jax.ShapeDtypeStruct((groups, rows, channels), BF),
            jax.ShapeDtypeStruct((groups, rows, 128), F32),
        ),
        in_specs=[anywhere] * 9 + [vmem] * 5,
        out_specs=(vmem, vmem),
        scratch_shapes=[
            pltpu.VMEM((FB, channels), BF),
            pltpu.VMEM((FB, channels), BF),
            *(pltpu.VMEM(table.shape, table.dtype) for table in tables),
            pltpu.VMEM((hidden, 128), F32),
            pltpu.VMEM((nz, NX, chunks, 2, CC, FB), BF),
            pltpu.VMEM((chunks, nz, 2, NX, CC, FB), BF),
            pltpu.VMEM((chunks, 2, nz, NX, CC, FB), BF),
            pltpu.VMEM((half, 2, CC, 2 * FB), BF),
            pltpu.VMEM((2 * parts, CC, FB), BF),
            pltpu.VMEM((hidden, seq), F32),
            pltpu.VMEM((hidden, seq), BF),
            pltpu.VMEM((hidden, seq), F32),
            pltpu.VMEM((256, seq), BF),
            pltpu.VMEM((own, seq), F32),
            pltpu.VMEM((groups, 2 * rows, 128), F32),
            pltpu.VMEM((groups, 2 * rows, 128), F32),
            pltpu.VMEM((nz, 2 * rows, 128), F32),
            pltpu.VMEM((NX, nz, rows, 128), BF),
            pltpu.VMEM((NX, rows, 128), F32),
            pltpu.VMEM((groups, rows, channels), BF),
            pltpu.VMEM((groups, rows, 128), F32),
            pltpu.SemaphoreType.DMA((9,)),
            pltpu.SemaphoreType.DMA((3 * chunks,)),
            pltpu.SemaphoreType.DMA((chunks,)),
            pltpu.SemaphoreType.DMA((chunks,)),
            pltpu.SemaphoreType.DMA((12,)),
        ],
        compiler_params=pltpu.CompilerParams(
            collective_id=0, has_side_effects=True, vmem_limit_bytes=60 * 1024 * 1024
        ),
    )(
        inputs[0], grad_out[0], *tables, w_last.T,
        w_first.T, b_first, w_mid, b_mid, decay_rate,
    )
    count = hidden * (order + hidden + 2) + channels * hidden
    first, first_bias, mid, mid_bias, last = pl.pallas_call(
        functools.partial(clip_kernel, count),
        out_shape=(
            jax.ShapeDtypeStruct((order, hidden), F32),
            jax.ShapeDtypeStruct((hidden,), F32),
            jax.ShapeDtypeStruct((hidden, hidden), F32),
            jax.ShapeDtypeStruct((hidden,), F32),
            jax.ShapeDtypeStruct((hidden, channels), F32),
        ),
        in_specs=[vmem] * 2,
        out_specs=(vmem,) * 5,
    )(last, small)
    return (first.T, first_bias, mid, mid_bias, last.T)


def solution(mesh):
    in_specs = (P("dp", "ctx", None), P("dp", "ctx", None), P(), P(), P(), P(), P(), P())
    out_specs = (P(), P(), P(), P(), P())
    return jax.shard_map(
        on_device, mesh=mesh, in_specs=in_specs, out_specs=out_specs, check_vma=False
    )
```

```python
import functools
import math

import jax
import jax.numpy as jnp
import ml_dtypes
import numpy as np
from jax import lax
from jax.experimental import pallas as pl
from jax.experimental.pallas import tpu as pltpu
from jax.sharding import PartitionSpec as P

BANDS = 16
FB = 256
CC = 16
BF = jnp.bfloat16
F32 = jnp.float32
MESH = pl.DeviceIdType.MESH
FP = 48
SPAN = 2048
NX = 4
PI_HIGH = 1.570770263671875
PI_LOW = math.pi / 2 - PI_HIGH


def make_tables(rows):
    seq = rows * FB
    half = rows + 1
    j = np.arange(half, dtype=np.int64)
    n = np.arange(rows, dtype=np.int64)
    m = np.arange(FB, dtype=np.int64)
    f32, bf = np.float32, ml_dtypes.bfloat16
    ang = (f32(math.pi) * (j[:, None] * n[None, :] % (2 * rows)).astype(f32) / f32(rows)).astype(f32)
    fr = np.cos(ang).astype(bf).astype(f32)
    fi = (-np.sin(ang)).astype(bf).astype(f32)
    ang = (f32(2.0 * math.pi) * (m[:, None] * m[None, :] % FB).astype(f32) / f32(FB)).astype(f32)
    er = np.cos(ang).astype(bf).astype(f32)
    ei = (-np.sin(ang)).astype(bf).astype(f32)
    ang = (f32(math.pi) * (j[:, None] * m[None, :] % (2 * seq)).astype(f32) / f32(seq)).astype(f32)
    tw = np.stack([np.cos(ang), -np.sin(ang)]).astype(f32)
    eye = np.eye(CC, dtype=f32)
    by_x = n.reshape(rows // NX, NX).T.reshape(-1)
    forward = np.kron(np.concatenate([fr, fi], 0)[:, by_x], eye).astype(bf)
    e_fwd = np.block([[er.T, ei.T], [-ei.T, er.T]]).astype(bf)
    e_inv = np.block([[er.T, -ei.T], [ei.T, er.T]]).astype(bf)
    twice = np.where(j % rows == 0, 1.0, 2.0).astype(f32)[:, None]
    both = np.concatenate([fr * twice, (fi * twice)[1:rows]], 0) * f32(0.5 / seq)
    inverse = np.kron(both.T, eye).astype(bf)
    q = np.arange(seq, dtype=np.int64)
    band = np.arange(1, BANDS + 1, dtype=np.int64)[:, None]
    ang = (f32(2.0 * math.pi) * (band * q[None, :] % seq).astype(f32) / f32(seq)).astype(f32)
    ramp = (q[None, :].astype(f32) / f32(seq)).astype(f32)
    feats = np.concatenate([ramp, np.cos(ang), np.sin(ang)], 0).astype(f32)
    high = feats.astype(bf)
    low = (feats - high.astype(f32)).astype(bf)
    zero = np.zeros((FP - feats.shape[0], seq), bf)
    ones = zero.copy()
    ones[0] = 1
    stack = np.concatenate([high, ones, low, zero], 0)
    return forward, e_fwd, e_inv, inverse, tw, stack


def nt(left, right):
    return lax.dot_general(left, right, (((1,), (1,)), ((), ())), preferred_element_type=F32)


def mm(left, right):
    return jnp.dot(left, right, preferred_element_type=F32)


def halves(value):
    high = value.astype(BF).astype(F32)
    return high, value - high


def column(row):
    n = row.shape[1]
    on = lax.broadcasted_iota(jnp.int32, (n, n), 0) == lax.broadcasted_iota(jnp.int32, (n, n), 1)
    return jnp.sum(jnp.where(on, jnp.broadcast_to(row, (n, n)), 0.0), axis=1, keepdims=True)


def sin_cos(value):
    turns = jnp.floor(value * (2.0 / math.pi) + 0.5)
    rest = (value - turns * PI_HIGH) - turns * PI_LOW
    square = rest * rest
    sine = rest + rest * square * (
        -1.6666654611e-1 + square * (8.3321608736e-3 + square * -1.9515295891e-4)
    )
    cosine = (1.0 - 0.5 * square) + square * square * (
        4.166664568298827e-2 + square * (-1.388731625493765e-3 + square * 2.443315711809948e-5)
    )
    quarter = turns.astype(jnp.int32)
    swap = (quarter & 1) == 1
    first = jnp.where(swap, cosine, sine)
    second = jnp.where(swap, sine, cosine)
    return (
        jnp.where((quarter & 2) == 2, -first, first),
        jnp.where(((quarter + 1) & 2) == 2, -second, second),
    )


def ahead(place, step, count):
    there = place + step
    return jnp.where(there >= count, there - count, there)


def behind(place, step, count):
    there = place - step
    return jnp.where(there < 0, there + count, there)


def main_kernel(
    parts, groups,
    x_any, g_any, fwd_any, ef_any, ei_any, inv_any, tw_any, feats_any, wl_any,
    wf_ref, bf_ref, wm_ref, bm_ref, rate_ref,
    last_ref, small_ref,
    x_ref, g_ref, fwd_ref, ef_ref, ei_ref, inv_ref, tw_ref, feats_ref, wl_ref,
    send, relay, recv, spec, back, cos_first, act_second, cos_second, wide, modul,
    part, got, ring, fin, small,
    load_sem, send_sem, relay_sem, recv_sem, sems,
):
    ctx = lax.axis_index("ctx")
    dp = lax.axis_index("dp")
    channels = x_ref.shape[1]
    own = channels // parts
    chunks = own // CC
    half = parts + 1
    order, hidden = wf_ref.shape
    seq = cos_first.shape[1]
    pair = 128 // own

    lanes_own = pl.ds(pl.multiple_of((ctx // pair) * 128, 128), 128)
    loads = [
        pltpu.make_async_copy(source, target, load_sem.at[i])
        for i, (source, target) in enumerate(
            (
                (x_any, x_ref), (g_any, g_ref), (wl_any.at[:, lanes_own], wl_ref), (feats_any, feats_ref),
                (tw_any, tw_ref), (fwd_any, fwd_ref), (ef_any, ef_ref), (ei_any, ei_ref), (inv_any, inv_ref),
            )
        )
    ]
    for load in loads:
        load.start()

    nz = parts // NX
    z, x = ctx // NX, lax.rem(ctx, NX)
    round_x = [ahead(x, r, NX) for r in range(NX)]
    round_z = [ahead(z, r, nz) for r in range(nz)]
    round_dp = [ahead(dp, r, groups) for r in range(groups)]
    peers_x = [{"ctx": z * NX + t} for t in round_x]
    peers_z = [{"ctx": t * NX + x} for t in round_z]
    peers_dp = [{"dp": t} for t in round_dp]

    barrier = pltpu.get_barrier_semaphore()
    for peer in peers_z[1:] + peers_x[1:] + peers_dp[1:]:
        pl.semaphore_signal(barrier, inc=1, device_id=peer, device_id_type=MESH)

    loads[0].wait()
    loads[1].wait()

    @pl.loop(0, channels // 128)
    def _(e):
        lanes = pl.ds(pl.multiple_of(e * 128, 128), 128)
        for v, ref in enumerate((x_ref, g_ref)):
            turned = ref[:, lanes].T
            for a in range(pair):
                to_z = (e * pair) // NX
                to_x = lax.rem(e * pair, NX) + a
                for k in range(chunks):
                    row = a * own + k * CC
                    send[to_z, to_x, k, v] = turned[row : row + CC]

    pl.semaphore_wait(barrier, nz + NX + groups - 3)

    def start(source, target, first, second, peer):
        pltpu.make_async_remote_copy(
            src_ref=source, dst_ref=target, send_sem=first, recv_sem=second,
            device_id=peer, device_id_type=MESH,
        ).start()

    for k in range(chunks):
        for r in range(1, NX):
            start(
                send.at[:, round_x[r], k], relay.at[k, :, :, NX - r], send_sem.at[k], relay_sem.at[k], peers_x[r]
            )
        for r in range(1, nz):
            start(
                send.at[round_z[r], x, k], recv.at[k, :, z, 0], send_sem.at[chunks + k], recv_sem.at[k], peers_z[r]
            )

    for k in range(chunks):
        recv[k, :, z, 0] = send[z, x, k]

    def forward(k):
        landed = relay.at[k, :, :, 1:]
        pltpu.make_async_copy(landed, landed, relay_sem.at[k]).wait()
        for r in range(1, nz):
            start(
                relay.at[k, round_z[r], :, 1:], recv.at[k, :, z, 1:], send_sem.at[2 * chunks + k], recv_sem.at[k],
                peers_z[r],
            )
        recv[k, :, z, 1:] = relay[k, z, :, 1:]

    for load in loads[2:]:
        load.wait()
    width = 512
    top = 256 - own
    wf = jnp.concatenate([wf_ref[...], jnp.zeros((FP - order, hidden), F32)], axis=0)
    wf_high, wf_low = halves(wf)
    wf_stack = jnp.concatenate([wf_high, wf_high, wf_low], axis=0).T.astype(BF)
    wm_high, wm_low = halves(wm_ref[...])
    wm_stack = jnp.concatenate([wm_high.T, wm_high.T, wm_low.T], axis=0).T.astype(BF)
    first_bias = column(bf_ref[...].reshape(1, hidden))
    second_bias = column(bm_ref[...].reshape(1, hidden))
    odd = lax.rem(ctx, pair) == 1
    rates = rate_ref[lanes_own].reshape(1, 128)
    rates = jnp.where(odd, pltpu.roll(jnp.broadcast_to(rates, (8, 128)), own, 1)[:1], rates)
    decay = column(rates[:, :own])
    wide[hidden : hidden + FP] = feats_ref[:FP]
    wide[hidden + FP : 128] = jnp.zeros((128 - hidden - FP, seq), BF)
    wide[128 : 128 + FP] = feats_ref[FP:]
    wide[128 + FP : top] = jnp.zeros((top - 128 - FP, seq), BF)

    def network(i):
        at = pl.ds(pl.multiple_of(i * width, width), width)
        high = feats_ref[:FP, at]
        stack = jnp.concatenate([high, feats_ref[FP:, at], high], axis=0)
        first, cos_one = sin_cos(mm(wf_stack, stack) + first_bias)
        cos_first[:, at] = cos_one
        high, low = halves(first)
        high, low = high.astype(BF), low.astype(BF)
        wide[:hidden, at] = high
        stack = jnp.concatenate([high, low, high], axis=0)
        second, cos_two = sin_cos(mm(wm_stack, stack) + second_bias)
        act_second[:, at] = second.astype(BF)
        cos_second[:, at] = cos_two
        places = (i * width + lax.broadcasted_iota(jnp.int32, (1, width), 1)).astype(F32)
        modul[:, at] = jnp.exp(-(decay * places) / seq)

    steps = seq // width
    pl.loop(0, steps * 3 // 4)(network)
    forward(0)
    pl.loop(steps * 3 // 4, steps)(network)
    for k in range(1, chunks):
        forward(k)

    def transform(k):
        landed = recv.at[k, :, : nz - 1]
        pltpu.make_async_copy(landed, landed, recv_sem.at[k]).wait()
        turn_re = tw_ref[0][:, None, :]
        turn_im = tw_ref[1][:, None, :]
        for v in range(2):
            columns = [
                recv[k, v, :, behind(t, x, NX)].reshape(nz * CC, FB) for t in range(NX)
            ]
            part_all = mm(fwd_ref[...], jnp.concatenate(columns, axis=0))
            part_re = part_all[: half * CC].reshape(half, CC, FB)
            part_im = part_all[half * CC :].reshape(half, CC, FB)
            spec[:, v, :, :FB] = (part_re * turn_re - part_im * turn_im).astype(BF)
            spec[:, v, :, FB:] = (part_re * turn_im + part_im * turn_re).astype(BF)
        both = mm(spec[...].reshape(half * 2 * CC, 2 * FB), ef_ref[...]).reshape(half, 2, CC, 2 * FB)
        x_re, x_im = both[:, 0, :, :FB], both[:, 0, :, FB:]
        g_re, g_im = both[:, 1, :, :FB], both[:, 1, :, FB:]
        cross = jnp.concatenate(
            [(x_re * g_re + x_im * g_im).astype(BF), (x_re * g_im - x_im * g_re).astype(BF)], axis=-1
        )
        inner = mm(cross.reshape(half * CC, 2 * FB), ei_ref[...]).reshape(half, CC, 2 * FB)
        in_re, in_im = inner[:, :, :FB], inner[:, :, FB:]
        back[:half] = (in_re * turn_re + in_im * turn_im).astype(BF)
        back[half:] = (in_im * turn_re - in_re * turn_im)[1:parts].astype(BF)
        grad = mm(inv_ref[...], back[...].reshape(2 * parts * CC, FB))
        first_row = k * CC if isinstance(k, int) else pl.multiple_of(k * CC, CC)
        for s in range(parts):
            at = slice(s * FB, (s + 1) * FB)
            wide[pl.ds(top + first_row, CC), at] = (
                grad[s * CC : (s + 1) * CC] * modul[pl.ds(first_row, CC), at]
            ).astype(BF)

    pl.loop(0, chunks - 1)(transform)
    transform(chunks - 1)

    span = SPAN
    tile = jnp.where(odd, pltpu.roll(wl_ref[...], own, 1), wl_ref[...])[:, :own]
    high, low = halves(tile.T)
    wl_stack = jnp.concatenate([high, low], axis=0).T.astype(BF)
    wmt_stack = jnp.concatenate([wm_high, wm_low], axis=0).T.astype(BF)
    total = jnp.zeros((3 * hidden, 256), F32)
    for i in range(seq // span):
        at = slice(i * span, (i + 1) * span)
        sh = wide[top:, at]
        d_second = (mm(wl_stack, jnp.concatenate([sh, sh], axis=0)) * cos_second[:, at]).astype(BF)
        d_first = (
            mm(wmt_stack, jnp.concatenate([d_second, d_second], axis=0)) * cos_first[:, at]
        ).astype(BF)
        lines = jnp.concatenate([d_second, d_first, act_second[:, at]], axis=0)
        total = total + nt(lines, wide[:, at])

    rows = hidden // groups
    lane = lax.broadcasted_iota(jnp.int32, (hidden, 128), 1)
    by_second, by_first = total[:hidden], total[hidden : 2 * hidden]
    at_bias = hidden + order
    mixed = by_first[:, :128] + pltpu.roll(by_first[:, 128:], hidden, 1)
    mixed = jnp.where(lane < hidden, by_second[:, :128], mixed)
    mixed = jnp.where(lane == at_bias + 1, pltpu.roll(by_second[:, :128], 1, 1), mixed)
    mixed = jnp.where(lane > at_bias + 1, 0.0, mixed)
    last = total[2 * hidden :, 128:]
    last = jnp.where(odd, last, pltpu.roll(last, own, 1))
    part[:, :rows] = last.reshape(groups, rows, 128)
    part[:, rows:] = mixed.reshape(groups, rows, 128)

    def wait(ref, which):
        pltpu.make_async_copy(ref, ref, sems.at[which]).wait()

    for r in range(1, groups):
        start(part.at[round_dp[r]], got.at[groups - r], sems.at[0], sems.at[1], peers_dp[r])
    wait(got.at[1:groups], 1)
    summed = part[dp]
    for r in range(1, groups):
        summed = summed + got[r]
    ring[0] = summed.astype(BF)

    for r in range(1, parts):
        start(ring.at[0], ring.at[parts - r], sems.at[2], sems.at[3], {"ctx": ahead(ctx, r, parts)})
    wait(ring.at[1:parts], 3)
    low_lanes = lax.broadcasted_iota(jnp.int32, (rows, 128), 1) < own
    summed = jnp.zeros((rows, 128), F32)
    for t in range(0, parts, 2):
        one = ring[behind(t, ctx, parts)].astype(F32)
        two = ring[behind(t + 1, ctx, parts)].astype(F32)
        fin[dp, :, t * own : t * own + 128] = jnp.where(low_lanes, one[:rows], two[:rows]).astype(BF)
        summed = summed + (one[rows:] + two[rows:])
    small[dp] = summed

    for r in range(1, groups):
        start(fin.at[dp], fin.at[dp], sems.at[4], sems.at[5], peers_dp[r])
        start(small.at[dp], small.at[dp], sems.at[6], sems.at[7], peers_dp[r])
    wait(fin.at[: groups - 1], 5)
    wait(small.at[: groups - 1], 7)
    last_ref[...] = fin[...]
    small_ref[...] = small[...]

    wait(got.at[1:groups], 0)
    wait(ring.at[1:parts], 2)
    wait(fin.at[: groups - 1], 4)
    wait(small.at[: groups - 1], 6)
    for k in range(chunks):
        for i, ref in enumerate((relay.at[k, :, :, 1:], recv.at[k, :, : nz - 1, 0], recv.at[k, :, : nz - 1, 1:])):
            pltpu.make_async_copy(ref, ref, send_sem.at[i * chunks + k]).wait()


def clip_kernel(count, last_in, small_in, first_ref, first_bias_ref, mid_ref, mid_bias_ref, last_ref):
    groups, rows, channels = last_in.shape
    hidden = groups * rows
    order = first_ref.shape[0]
    grads = last_in[...].astype(F32)
    others = small_in[...].reshape(hidden, 128)
    squares = jnp.sum(jnp.sum(grads * grads, axis=0), keepdims=True) + jnp.sum(others * others, keepdims=True)
    factor = jnp.minimum(1.0, math.sqrt(count) / (jnp.sqrt(squares) + 1e-06))
    last_ref[...] = grads.reshape(hidden, channels) * factor
    others = others * factor
    mid_ref[...] = others[:, :hidden]
    turned = others.T
    first_ref[...] = turned[hidden : hidden + order]
    first_bias_ref[...] = turned[hidden + order]
    mid_bias_ref[...] = turned[hidden + order + 1]


def on_device(inputs, grad_out, w_first, b_first, w_mid, b_mid, w_last, decay_rate):
    parts = lax.axis_size("ctx")
    groups = lax.axis_size("dp")
    channels = inputs.shape[2]
    hidden, order = w_first.shape
    own = channels // parts
    chunks = own // CC
    half = parts + 1
    seq = parts * FB
    rows = hidden // groups
    nz = parts // NX
    tables = make_tables(parts)
    vmem = pl.BlockSpec(memory_space=pltpu.VMEM)
    anywhere = pl.BlockSpec(memory_space=pl.ANY)
    last, small = pl.pallas_call(
        functools.partial(main_kernel, parts, groups),
        out_shape=(
            jax.ShapeDtypeStruct((groups, rows, channels), BF),
            jax.ShapeDtypeStruct((groups, rows, 128), F32),
        ),
        in_specs=[anywhere] * 9 + [vmem] * 5,
        out_specs=(vmem, vmem),
        scratch_shapes=[
            pltpu.VMEM((FB, channels), BF),
            pltpu.VMEM((FB, channels), BF),
            *(pltpu.VMEM(table.shape, table.dtype) for table in tables),
            pltpu.VMEM((hidden, 128), F32),
            pltpu.VMEM((nz, NX, chunks, 2, CC, FB), BF),
            pltpu.VMEM((chunks, nz, 2, NX, CC, FB), BF),
            pltpu.VMEM((chunks, 2, nz, NX, CC, FB), BF),
            pltpu.VMEM((half, 2, CC, 2 * FB), BF),
            pltpu.VMEM((2 * parts, CC, FB), BF),
            pltpu.VMEM((hidden, seq), F32),
            pltpu.VMEM((hidden, seq), BF),
            pltpu.VMEM((hidden, seq), F32),
            pltpu.VMEM((256, seq), BF),
            pltpu.VMEM((own, seq), F32),
            pltpu.VMEM((groups, 2 * rows, 128), F32),
            pltpu.VMEM((groups, 2 * rows, 128), F32),
            pltpu.VMEM((parts, 2 * rows, 128), BF),
            pltpu.VMEM((groups, rows, channels), BF),
            pltpu.VMEM((groups, rows, 128), F32),
            pltpu.SemaphoreType.DMA((9,)),
            pltpu.SemaphoreType.DMA((3 * chunks,)),
            pltpu.SemaphoreType.DMA((chunks,)),
            pltpu.SemaphoreType.DMA((chunks,)),
            pltpu.SemaphoreType.DMA((8,)),
        ],
        compiler_params=pltpu.CompilerParams(
            collective_id=0, has_side_effects=True, vmem_limit_bytes=60 * 1024 * 1024
        ),
    )(
        inputs[0], grad_out[0], *tables, w_last.T,
        w_first.T, b_first, w_mid, b_mid, decay_rate,
    )
    count = hidden * (order + hidden + 2) + channels * hidden
    first, first_bias, mid, mid_bias, last = pl.pallas_call(
        functools.partial(clip_kernel, count),
        out_shape=(
            jax.ShapeDtypeStruct((order, hidden), F32),
            jax.ShapeDtypeStruct((hidden,), F32),
            jax.ShapeDtypeStruct((hidden, hidden), F32),
            jax.ShapeDtypeStruct((hidden,), F32),
            jax.ShapeDtypeStruct((hidden, channels), F32),
        ),
        in_specs=[vmem] * 2,
        out_specs=(vmem,) * 5,
    )(last, small)
    return (first.T, first_bias, mid, mid_bias, last.T)


def solution(mesh):
    in_specs = (P("dp", "ctx", None), P("dp", "ctx", None), P(), P(), P(), P(), P(), P())
    out_specs = (P(), P(), P(), P(), P())
    return jax.shard_map(
        on_device, mesh=mesh, in_specs=in_specs, out_specs=out_specs, check_vma=False
    )
```

```python
import functools
import math

import jax
import jax.numpy as jnp
import ml_dtypes
import numpy as np
from jax import lax
from jax.experimental import pallas as pl
from jax.experimental.pallas import tpu as pltpu
from jax.sharding import PartitionSpec as P

BANDS = 16
FB = 256
CC = 16
BF = jnp.bfloat16
F32 = jnp.float32
MESH = pl.DeviceIdType.MESH
FP = 48
SPAN = 2048
HALVES = 2
NX = 4
PI_HIGH = 1.570770263671875
PI_LOW = math.pi / 2 - PI_HIGH


def make_tables(rows):
    seq = rows * FB
    half = rows + 1
    j = np.arange(half, dtype=np.int64)
    n = np.arange(rows, dtype=np.int64)
    m = np.arange(FB, dtype=np.int64)
    f32, bf = np.float32, ml_dtypes.bfloat16
    ang = (f32(math.pi) * (j[:, None] * n[None, :] % (2 * rows)).astype(f32) / f32(rows)).astype(f32)
    fr = np.cos(ang).astype(bf).astype(f32)
    fi = (-np.sin(ang)).astype(bf).astype(f32)
    ang = (f32(2.0 * math.pi) * (m[:, None] * m[None, :] % FB).astype(f32) / f32(FB)).astype(f32)
    er = np.cos(ang).astype(bf).astype(f32)
    ei = (-np.sin(ang)).astype(bf).astype(f32)
    ang = (f32(math.pi) * (j[:, None] * m[None, :] % (2 * seq)).astype(f32) / f32(seq)).astype(f32)
    tw = np.stack([np.cos(ang), -np.sin(ang)]).astype(f32)
    eye = np.eye(CC, dtype=f32)
    by_x = n.reshape(rows // NX, NX).T.reshape(-1)
    forward = np.kron(np.concatenate([fr, fi], 0)[:, by_x], eye).astype(bf)
    e_fwd = np.block([[er.T, ei.T], [-ei.T, er.T]]).astype(bf)
    e_inv = np.block([[er.T, -ei.T], [ei.T, er.T]]).astype(bf)
    twice = np.where(j % rows == 0, 1.0, 2.0).astype(f32)[:, None]
    both = np.concatenate([fr * twice, (fi * twice)[1:rows]], 0) * f32(0.5 / seq)
    inverse = np.kron(both.T, eye).astype(bf)
    q = np.arange(seq, dtype=np.int64)
    band = np.arange(1, BANDS + 1, dtype=np.int64)[:, None]
    ang = (f32(2.0 * math.pi) * (band * q[None, :] % seq).astype(f32) / f32(seq)).astype(f32)
    ramp = (q[None, :].astype(f32) / f32(seq)).astype(f32)
    feats = np.concatenate([ramp, np.cos(ang), np.sin(ang)], 0).astype(f32)
    high = feats.astype(bf)
    low = (feats - high.astype(f32)).astype(bf)
    zero = np.zeros((FP - feats.shape[0], seq), bf)
    ones = zero.copy()
    ones[0] = 1
    stack = np.concatenate([high, ones, low, zero], 0)
    return forward, e_fwd, e_inv, inverse, tw, stack


def nt(left, right):
    return lax.dot_general(left, right, (((1,), (1,)), ((), ())), preferred_element_type=F32)


def mm(left, right):
    return jnp.dot(left, right, preferred_element_type=F32)


def halves(value):
    high = value.astype(BF).astype(F32)
    return high, value - high


def column(row):
    n = row.shape[1]
    on = lax.broadcasted_iota(jnp.int32, (n, n), 0) == lax.broadcasted_iota(jnp.int32, (n, n), 1)
    return jnp.sum(jnp.where(on, jnp.broadcast_to(row, (n, n)), 0.0), axis=1, keepdims=True)


def sin_cos(value):
    turns = jnp.floor(value * (2.0 / math.pi) + 0.5)
    rest = (value - turns * PI_HIGH) - turns * PI_LOW
    square = rest * rest
    sine = rest + rest * square * (
        -1.6666654611e-1 + square * (8.3321608736e-3 + square * -1.9515295891e-4)
    )
    cosine = (1.0 - 0.5 * square) + square * square * (
        4.166664568298827e-2 + square * (-1.388731625493765e-3 + square * 2.443315711809948e-5)
    )
    quarter = turns.astype(jnp.int32)
    swap = (quarter & 1) == 1
    first = jnp.where(swap, cosine, sine)
    second = jnp.where(swap, sine, cosine)
    return (
        jnp.where((quarter & 2) == 2, -first, first),
        jnp.where(((quarter + 1) & 2) == 2, -second, second),
    )


def ahead(place, step, count):
    there = place + step
    return jnp.where(there >= count, there - count, there)


def behind(place, step, count):
    there = place - step
    return jnp.where(there < 0, there + count, there)


def main_kernel(
    parts, groups,
    x_any, g_any, fwd_any, ef_any, ei_any, inv_any, tw_any, feats_any, wl_any,
    wf_any, bf_any, wm_any, bm_any, rate_any,
    last_ref, small_ref,
    x_ref, g_ref, fwd_ref, ef_ref, ei_ref, inv_ref, tw_ref, feats_ref, wl_ref,
    wf_ref, bf_ref, wm_ref, bm_ref, rate_ref,
    send, relay, recv, spec, back, cos_first, act_second, cos_second, wide, modul,
    part, got, ring, fin, small,
    block_sem, load_sem, send_sem, relay_sem, recv_sem, sems,
):
    ctx = lax.axis_index("ctx")
    dp = lax.axis_index("dp")
    channels = x_ref.shape[1]
    own = channels // parts
    chunks = own // CC
    half = parts + 1
    order, hidden = wf_ref.shape
    seq = cos_first.shape[1]
    pair = 128 // own

    lanes_own = pl.ds(pl.multiple_of((ctx // pair) * 128, 128), 128)
    parted = [pl.ds(i * (channels // HALVES), channels // HALVES) for i in range(HALVES)]
    blocks = [
        pltpu.make_async_copy(source.at[:, at], target.at[:, at], block_sem.at[2 * i + v])
        for i, at in enumerate(parted)
        for v, (source, target) in enumerate(((x_any, x_ref), (g_any, g_ref)))
    ]
    loads = [
        pltpu.make_async_copy(source, target, load_sem.at[i])
        for i, (source, target) in enumerate(
            (
                (wf_any, wf_ref), (bf_any, bf_ref), (wm_any, wm_ref), (bm_any, bm_ref), (rate_any, rate_ref),
                (wl_any.at[:, lanes_own], wl_ref), (feats_any, feats_ref), (tw_any, tw_ref),
                (fwd_any, fwd_ref), (ef_any, ef_ref), (ei_any, ei_ref), (inv_any, inv_ref),
            )
        )
    ]
    for load in blocks:
        load.start()

    nz = parts // NX
    z, x = ctx // NX, lax.rem(ctx, NX)
    round_x = [ahead(x, r, NX) for r in range(NX)]
    round_z = [ahead(z, r, nz) for r in range(nz)]
    round_dp = [ahead(dp, r, groups) for r in range(groups)]
    peers_x = [{"ctx": z * NX + t} for t in round_x]
    peers_z = [{"ctx": t * NX + x} for t in round_z]
    peers_dp = [{"dp": t} for t in round_dp]

    barrier = pltpu.get_barrier_semaphore()
    far_z = sorted(range(1, nz), key=lambda r: -min(r, nz - r))
    for peer in [peers_z[r] for r in far_z] + peers_x[1:] + peers_dp[1:]:
        pl.semaphore_signal(barrier, inc=1, device_id=peer, device_id_type=MESH)
    for load in loads:
        load.start()

    def turn(e):
        lanes = pl.ds(pl.multiple_of(e * 128, 128), 128)
        for v, ref in enumerate((x_ref, g_ref)):
            turned = ref[:, lanes].T
            for a in range(pair):
                to_z = (e * pair) // NX
                to_x = lax.rem(e * pair, NX) + a
                for k in range(chunks):
                    row = a * own + k * CC
                    send[to_z, to_x, k, v] = turned[row : row + CC]

    tiles = channels // 128 // HALVES
    for i in range(HALVES):
        blocks[2 * i].wait()
        blocks[2 * i + 1].wait()
        pl.loop(i * tiles, (i + 1) * tiles)(turn)

    pl.semaphore_wait(barrier, nz + NX + groups - 3)

    def start(source, target, first, second, peer):
        pltpu.make_async_remote_copy(
            src_ref=source, dst_ref=target, send_sem=first, recv_sem=second,
            device_id=peer, device_id_type=MESH,
        ).start()

    for k in range(chunks):
        for r in range(1, NX):
            start(
                send.at[:, round_x[r], k], relay.at[k, :, :, NX - r], send_sem.at[k], relay_sem.at[k], peers_x[r]
            )
        for r in range(1, nz):
            start(
                send.at[round_z[r], x, k], recv.at[k, :, z, 0], send_sem.at[chunks + k], recv_sem.at[k], peers_z[r]
            )

    for k in range(chunks):
        recv[k, :, z, 0] = send[z, x, k]

    def forward(k):
        landed = relay.at[k, :, :, 1:]
        pltpu.make_async_copy(landed, landed, relay_sem.at[k]).wait()
        for r in range(1, nz):
            start(
                relay.at[k, round_z[r], :, 1:], recv.at[k, :, z, 1:], send_sem.at[2 * chunks + k], recv_sem.at[k],
                peers_z[r],
            )
        recv[k, :, z, 1:] = relay[k, z, :, 1:]

    for load in loads:
        load.wait()
    width = 512
    top = 256 - own
    wf = jnp.concatenate([wf_ref[...], jnp.zeros((FP - order, hidden), F32)], axis=0)
    wf_high, wf_low = halves(wf)
    wf_stack = jnp.concatenate([wf_high, wf_high, wf_low], axis=0).T.astype(BF)
    wm_high, wm_low = halves(wm_ref[...])
    wm_stack = jnp.concatenate([wm_high.T, wm_high.T, wm_low.T], axis=0).T.astype(BF)
    first_bias = column(bf_ref[...].reshape(1, hidden))
    second_bias = column(bm_ref[...].reshape(1, hidden))
    odd = lax.rem(ctx, pair) == 1
    rates = rate_ref[lanes_own].reshape(1, 128)
    rates = jnp.where(odd, pltpu.roll(jnp.broadcast_to(rates, (8, 128)), own, 1)[:1], rates)
    decay = column(rates[:, :own])
    wide[hidden : hidden + FP] = feats_ref[:FP]
    wide[hidden + FP : 128] = jnp.zeros((128 - hidden - FP, seq), BF)
    wide[128 : 128 + FP] = feats_ref[FP:]
    wide[128 + FP : top] = jnp.zeros((top - 128 - FP, seq), BF)

    def network(i):
        at = pl.ds(pl.multiple_of(i * width, width), width)
        high = feats_ref[:FP, at]
        stack = jnp.concatenate([high, feats_ref[FP:, at], high], axis=0)
        first, cos_one = sin_cos(mm(wf_stack, stack) + first_bias)
        cos_first[:, at] = cos_one
        high, low = halves(first)
        high, low = high.astype(BF), low.astype(BF)
        wide[:hidden, at] = high
        stack = jnp.concatenate([high, low, high], axis=0)
        second, cos_two = sin_cos(mm(wm_stack, stack) + second_bias)
        act_second[:, at] = second.astype(BF)
        cos_second[:, at] = cos_two
        places = (i * width + lax.broadcasted_iota(jnp.int32, (1, width), 1)).astype(F32)
        modul[:, at] = jnp.exp(-(decay * places) / seq)

    steps = seq // width
    pl.loop(0, steps * 3 // 4)(network)
    forward(0)
    pl.loop(steps * 3 // 4, steps)(network)
    for k in range(1, chunks):
        forward(k)

    def transform(k):
        landed = recv.at[k, :, : nz - 1]
        pltpu.make_async_copy(landed, landed, recv_sem.at[k]).wait()
        turn_re = tw_ref[0][:, None, :]
        turn_im = tw_ref[1][:, None, :]
        for v in range(2):
            columns = [
                recv[k, v, :, behind(t, x, NX)].reshape(nz * CC, FB) for t in range(NX)
            ]
            part_all = mm(fwd_ref[...], jnp.concatenate(columns, axis=0))
            part_re = part_all[: half * CC].reshape(half, CC, FB)
            part_im = part_all[half * CC :].reshape(half, CC, FB)
            spec[:, v, :, :FB] = (part_re * turn_re - part_im * turn_im).astype(BF)
            spec[:, v, :, FB:] = (part_re * turn_im + part_im * turn_re).astype(BF)
        both = mm(spec[...].reshape(half * 2 * CC, 2 * FB), ef_ref[...]).reshape(half, 2, CC, 2 * FB)
        x_re, x_im = both[:, 0, :, :FB], both[:, 0, :, FB:]
        g_re, g_im = both[:, 1, :, :FB], both[:, 1, :, FB:]
        cross = jnp.concatenate(
            [(x_re * g_re + x_im * g_im).astype(BF), (x_re * g_im - x_im * g_re).astype(BF)], axis=-1
        )
        inner = mm(cross.reshape(half * CC, 2 * FB), ei_ref[...]).reshape(half, CC, 2 * FB)
        in_re, in_im = inner[:, :, :FB], inner[:, :, FB:]
        back[:half] = (in_re * turn_re + in_im * turn_im).astype(BF)
        back[half:] = (in_im * turn_re - in_re * turn_im)[1:parts].astype(BF)
        grad = mm(inv_ref[...], back[...].reshape(2 * parts * CC, FB))
        first_row = k * CC if isinstance(k, int) else pl.multiple_of(k * CC, CC)
        for s in range(parts):
            at = slice(s * FB, (s + 1) * FB)
            wide[pl.ds(top + first_row, CC), at] = (
                grad[s * CC : (s + 1) * CC] * modul[pl.ds(first_row, CC), at]
            ).astype(BF)

    pl.loop(0, chunks - 1)(transform)
    transform(chunks - 1)

    span = SPAN
    tile = jnp.where(odd, pltpu.roll(wl_ref[...], own, 1), wl_ref[...])[:, :own]
    high, low = halves(tile.T)
    wl_stack = jnp.concatenate([high, low], axis=0).T.astype(BF)
    wmt_stack = jnp.concatenate([wm_high, wm_low], axis=0).T.astype(BF)
    total = jnp.zeros((3 * hidden, 256), F32)
    for i in range(seq // span):
        at = slice(i * span, (i + 1) * span)
        sh = wide[top:, at]
        d_second = (mm(wl_stack, jnp.concatenate([sh, sh], axis=0)) * cos_second[:, at]).astype(BF)
        d_first = (
            mm(wmt_stack, jnp.concatenate([d_second, d_second], axis=0)) * cos_first[:, at]
        ).astype(BF)
        lines = jnp.concatenate([d_second, d_first, act_second[:, at]], axis=0)
        total = total + nt(lines, wide[:, at])

    rows = hidden // groups
    lane = lax.broadcasted_iota(jnp.int32, (hidden, 128), 1)
    by_second, by_first = total[:hidden], total[hidden : 2 * hidden]
    at_bias = hidden + order
    mixed = by_first[:, :128] + pltpu.roll(by_first[:, 128:], hidden, 1)
    mixed = jnp.where(lane < hidden, by_second[:, :128], mixed)
    mixed = jnp.where(lane == at_bias + 1, pltpu.roll(by_second[:, :128], 1, 1), mixed)
    mixed = jnp.where(lane > at_bias + 1, 0.0, mixed)
    last = total[2 * hidden :, 128:]
    last = jnp.where(odd, last, pltpu.roll(last, own, 1))
    part[:, :rows] = last.reshape(groups, rows, 128)
    part[:, rows:] = mixed.reshape(groups, rows, 128)

    def wait(ref, which):
        pltpu.make_async_copy(ref, ref, sems.at[which]).wait()

    for r in range(1, groups):
        start(part.at[round_dp[r]], got.at[groups - r], sems.at[0], sems.at[1], peers_dp[r])
    wait(got.at[1:groups], 1)
    summed = part[dp]
    for r in range(1, groups):
        summed = summed + got[r]
    ring[0] = summed.astype(BF)

    for r in range(1, parts):
        start(ring.at[0], ring.at[parts - r], sems.at[2], sems.at[3], {"ctx": ahead(ctx, r, parts)})
    wait(ring.at[1:parts], 3)
    low_lanes = lax.broadcasted_iota(jnp.int32, (rows, 128), 1) < own
    summed = jnp.zeros((rows, 128), F32)
    for t in range(0, parts, 2):
        one = ring[behind(t, ctx, parts)].astype(F32)
        two = ring[behind(t + 1, ctx, parts)].astype(F32)
        fin[dp, :, t * own : t * own + 128] = jnp.where(low_lanes, one[:rows], two[:rows]).astype(BF)
        summed = summed + (one[rows:] + two[rows:])
    small[dp] = summed

    for r in range(1, groups):
        start(fin.at[dp], fin.at[dp], sems.at[4], sems.at[5], peers_dp[r])
        start(small.at[dp], small.at[dp], sems.at[6], sems.at[7], peers_dp[r])
    wait(fin.at[: groups - 1], 5)
    wait(small.at[: groups - 1], 7)
    last_ref[...] = fin[...]
    small_ref[...] = small[...]

    wait(got.at[1:groups], 0)
    wait(ring.at[1:parts], 2)
    wait(fin.at[: groups - 1], 4)
    wait(small.at[: groups - 1], 6)
    for k in range(chunks):
        for i, ref in enumerate((relay.at[k, :, :, 1:], recv.at[k, :, : nz - 1, 0], recv.at[k, :, : nz - 1, 1:])):
            pltpu.make_async_copy(ref, ref, send_sem.at[i * chunks + k]).wait()


def clip_kernel(count, last_in, small_in, first_ref, first_bias_ref, mid_ref, mid_bias_ref, last_ref):
    groups, rows, channels = last_in.shape
    hidden = groups * rows
    order = first_ref.shape[0]
    grads = last_in[...].astype(F32)
    others = small_in[...].reshape(hidden, 128)
    squares = jnp.sum(jnp.sum(grads * grads, axis=0), keepdims=True) + jnp.sum(others * others, keepdims=True)
    factor = jnp.minimum(1.0, math.sqrt(count) / (jnp.sqrt(squares) + 1e-06))
    last_ref[...] = grads.reshape(hidden, channels) * factor
    others = others * factor
    mid_ref[...] = others[:, :hidden]
    turned = others.T
    first_ref[...] = turned[hidden : hidden + order]
    first_bias_ref[...] = turned[hidden + order]
    mid_bias_ref[...] = turned[hidden + order + 1]


def on_device(inputs, grad_out, w_first, b_first, w_mid, b_mid, w_last, decay_rate):
    parts = lax.axis_size("ctx")
    groups = lax.axis_size("dp")
    channels = inputs.shape[2]
    hidden, order = w_first.shape
    own = channels // parts
    chunks = own // CC
    half = parts + 1
    seq = parts * FB
    rows = hidden // groups
    nz = parts // NX
    tables = make_tables(parts)
    vmem = pl.BlockSpec(memory_space=pltpu.VMEM)
    anywhere = pl.BlockSpec(memory_space=pl.ANY)
    last, small = pl.pallas_call(
        functools.partial(main_kernel, parts, groups),
        out_shape=(
            jax.ShapeDtypeStruct((groups, rows, channels), BF),
            jax.ShapeDtypeStruct((groups, rows, 128), F32),
        ),
        in_specs=[anywhere] * 14,
        out_specs=(vmem, vmem),
        scratch_shapes=[
            pltpu.VMEM((FB, channels), BF),
            pltpu.VMEM((FB, channels), BF),
            *(pltpu.VMEM(table.shape, table.dtype) for table in tables),
            pltpu.VMEM((hidden, 128), F32),
            pltpu.VMEM((order, hidden), F32),
            pltpu.VMEM((hidden,), F32),
            pltpu.VMEM((hidden, hidden), F32),
            pltpu.VMEM((hidden,), F32),
            pltpu.VMEM((channels,), F32),
            pltpu.VMEM((nz, NX, chunks, 2, CC, FB), BF),
            pltpu.VMEM((chunks, nz, 2, NX, CC, FB), BF),
            pltpu.VMEM((chunks, 2, nz, NX, CC, FB), BF),
            pltpu.VMEM((half, 2, CC, 2 * FB), BF),
            pltpu.VMEM((2 * parts, CC, FB), BF),
            pltpu.VMEM((hidden, seq), F32),
            pltpu.VMEM((hidden, seq), BF),
            pltpu.VMEM((hidden, seq), F32),
            pltpu.VMEM((256, seq), BF),
            pltpu.VMEM((own, seq), F32),
            pltpu.VMEM((groups, 2 * rows, 128), F32),
            pltpu.VMEM((groups, 2 * rows, 128), F32),
            pltpu.VMEM((parts, 2 * rows, 128), BF),
            pltpu.VMEM((groups, rows, channels), BF),
            pltpu.VMEM((groups, rows, 128), F32),
            pltpu.SemaphoreType.DMA((2 * HALVES,)),
            pltpu.SemaphoreType.DMA((12,)),
            pltpu.SemaphoreType.DMA((3 * chunks,)),
            pltpu.SemaphoreType.DMA((chunks,)),
            pltpu.SemaphoreType.DMA((chunks,)),
            pltpu.SemaphoreType.DMA((8,)),
        ],
        compiler_params=pltpu.CompilerParams(
            collective_id=0, has_side_effects=True, vmem_limit_bytes=60 * 1024 * 1024
        ),
    )(
        inputs[0], grad_out[0], *tables, w_last.T,
        w_first.T, b_first, w_mid, b_mid, decay_rate,
    )
    count = hidden * (order + hidden + 2) + channels * hidden
    first, first_bias, mid, mid_bias, last = pl.pallas_call(
        functools.partial(clip_kernel, count),
        out_shape=(
            jax.ShapeDtypeStruct((order, hidden), F32),
            jax.ShapeDtypeStruct((hidden,), F32),
            jax.ShapeDtypeStruct((hidden, hidden), F32),
            jax.ShapeDtypeStruct((hidden,), F32),
            jax.ShapeDtypeStruct((hidden, channels), F32),
        ),
        in_specs=[vmem] * 2,
        out_specs=(vmem,) * 5,
    )(last, small)
    return (first.T, first_bias, mid, mid_bias, last.T)


def solution(mesh):
    in_specs = (P("dp", "ctx", None), P("dp", "ctx", None), P(), P(), P(), P(), P(), P())
    out_specs = (P(), P(), P(), P(), P())
    return jax.shard_map(
        on_device, mesh=mesh, in_specs=in_specs, out_specs=out_specs, check_vma=False
    )
```

```python
import functools
import math

import jax
import jax.numpy as jnp
import ml_dtypes
import numpy as np
from jax import lax
from jax.experimental import pallas as pl
from jax.experimental.pallas import tpu as pltpu
from jax.sharding import PartitionSpec as P

BANDS = 16
FB = 256
CC = 16
BF = jnp.bfloat16
F32 = jnp.float32
MESH = pl.DeviceIdType.MESH
FP = 48
SPAN = 2048
HALVES = 2
NX = 4
PI_HIGH = 1.570770263671875
PI_LOW = math.pi / 2 - PI_HIGH


def make_tables(rows):
    seq = rows * FB
    half = rows + 1
    j = np.arange(half, dtype=np.int64)
    n = np.arange(rows, dtype=np.int64)
    m = np.arange(FB, dtype=np.int64)
    f32, bf = np.float32, ml_dtypes.bfloat16
    ang = (f32(math.pi) * (j[:, None] * n[None, :] % (2 * rows)).astype(f32) / f32(rows)).astype(f32)
    fr = np.cos(ang).astype(bf).astype(f32)
    fi = (-np.sin(ang)).astype(bf).astype(f32)
    ang = (f32(2.0 * math.pi) * (m[:, None] * m[None, :] % FB).astype(f32) / f32(FB)).astype(f32)
    er = np.cos(ang).astype(bf).astype(f32)
    ei = (-np.sin(ang)).astype(bf).astype(f32)
    ang = (f32(math.pi) * (j[:, None] * m[None, :] % (2 * seq)).astype(f32) / f32(seq)).astype(f32)
    tw = np.stack([np.cos(ang), -np.sin(ang)]).astype(f32)
    eye = np.eye(CC, dtype=f32)
    by_x = n.reshape(rows // NX, NX).T.reshape(-1)
    forward = np.kron(np.concatenate([fr, fi], 0)[:, by_x], eye).astype(bf)
    e_fwd = np.block([[er.T, ei.T], [-ei.T, er.T]]).astype(bf)
    e_inv = np.block([[er.T, -ei.T], [ei.T, er.T]]).astype(bf)
    twice = np.where(j % rows == 0, 1.0, 2.0).astype(f32)[:, None]
    both = np.concatenate([fr * twice, (fi * twice)[1:rows]], 0) * f32(0.5 / seq)
    inverse = np.kron(both.T, eye).astype(bf)
    q = np.arange(seq, dtype=np.int64)
    band = np.arange(1, BANDS + 1, dtype=np.int64)[:, None]
    ang = (f32(2.0 * math.pi) * (band * q[None, :] % seq).astype(f32) / f32(seq)).astype(f32)
    ramp = (q[None, :].astype(f32) / f32(seq)).astype(f32)
    feats = np.concatenate([ramp, np.cos(ang), np.sin(ang)], 0).astype(f32)
    high = feats.astype(bf)
    low = (feats - high.astype(f32)).astype(bf)
    zero = np.zeros((FP - feats.shape[0], seq), bf)
    ones = zero.copy()
    ones[0] = 1
    stack = np.concatenate([high, ones, low, zero], 0)
    return forward, e_fwd, e_inv, inverse, tw, stack


def nt(left, right):
    return lax.dot_general(left, right, (((1,), (1,)), ((), ())), preferred_element_type=F32)


def mm(left, right):
    return jnp.dot(left, right, preferred_element_type=F32)


def halves(value):
    high = value.astype(BF).astype(F32)
    return high, value - high


def column(row):
    n = row.shape[1]
    on = lax.broadcasted_iota(jnp.int32, (n, n), 0) == lax.broadcasted_iota(jnp.int32, (n, n), 1)
    return jnp.sum(jnp.where(on, jnp.broadcast_to(row, (n, n)), 0.0), axis=1, keepdims=True)


def sin_cos(value):
    turns = jnp.floor(value * (2.0 / math.pi) + 0.5)
    rest = (value - turns * PI_HIGH) - turns * PI_LOW
    square = rest * rest
    sine = rest + rest * square * (
        -1.6666654611e-1 + square * (8.3321608736e-3 + square * -1.9515295891e-4)
    )
    cosine = (1.0 - 0.5 * square) + square * square * (
        4.166664568298827e-2 + square * (-1.388731625493765e-3 + square * 2.443315711809948e-5)
    )
    quarter = turns.astype(jnp.int32)
    swap = (quarter & 1) == 1
    first = jnp.where(swap, cosine, sine)
    second = jnp.where(swap, sine, cosine)
    return (
        jnp.where((quarter & 2) == 2, -first, first),
        jnp.where(((quarter + 1) & 2) == 2, -second, second),
    )


def ahead(place, step, count):
    there = place + step
    return jnp.where(there >= count, there - count, there)


def behind(place, step, count):
    there = place - step
    return jnp.where(there < 0, there + count, there)


def main_kernel(
    parts, groups,
    x_any, g_any, fwd_any, ef_any, ei_any, inv_any, tw_any, feats_any, wl_any,
    wf_any, bf_any, wm_any, bm_any, rate_any,
    last_ref, small_ref,
    x_ref, g_ref, fwd_ref, ef_ref, ei_ref, inv_ref, tw_ref, feats_ref, wl_ref,
    wf_ref, bf_ref, wm_ref, bm_ref, rate_ref,
    send, relay, recv, spec, back, cos_first, act_second, cos_second, wide, modul,
    part, got, ring, fin, small,
    block_sem, load_sem, send_sem, relay_sem, recv_sem, sems, result_sem,
):
    ctx = lax.axis_index("ctx")
    dp = lax.axis_index("dp")
    channels = x_ref.shape[1]
    own = channels // parts
    chunks = own // CC
    half = parts + 1
    order, hidden = wf_ref.shape
    seq = cos_first.shape[1]
    pair = 128 // own

    lanes_own = pl.ds(pl.multiple_of((ctx // pair) * 128, 128), 128)
    parted = [pl.ds(i * (channels // HALVES), channels // HALVES) for i in range(HALVES)]
    blocks = [
        pltpu.make_async_copy(source.at[:, at], target.at[:, at], block_sem.at[2 * i + v])
        for i, at in enumerate(parted)
        for v, (source, target) in enumerate(((x_any, x_ref), (g_any, g_ref)))
    ]
    loads = [
        pltpu.make_async_copy(source, target, load_sem.at[i])
        for i, (source, target) in enumerate(
            (
                (wf_any, wf_ref), (bf_any, bf_ref), (wm_any, wm_ref), (bm_any, bm_ref), (rate_any, rate_ref),
                (wl_any.at[:, lanes_own], wl_ref), (feats_any, feats_ref), (tw_any, tw_ref),
                (fwd_any, fwd_ref), (ef_any, ef_ref), (ei_any, ei_ref), (inv_any, inv_ref),
            )
        )
    ]
    for load in blocks:
        load.start()

    nz = parts // NX
    z, x = ctx // NX, lax.rem(ctx, NX)
    round_x = [ahead(x, r, NX) for r in range(NX)]
    round_z = [ahead(z, r, nz) for r in range(nz)]
    round_dp = [ahead(dp, r, groups) for r in range(groups)]
    peers_x = [{"ctx": z * NX + t} for t in round_x]
    peers_z = [{"ctx": t * NX + x} for t in round_z]
    peers_dp = [{"dp": t} for t in round_dp]

    barrier = pltpu.get_barrier_semaphore()
    far_z = sorted(range(1, nz), key=lambda r: -min(r, nz - r))
    for peer in [peers_z[r] for r in far_z] + peers_x[1:] + peers_dp[1:]:
        pl.semaphore_signal(barrier, inc=1, device_id=peer, device_id_type=MESH)
    for load in loads:
        load.start()

    def turn(e):
        lanes = pl.ds(pl.multiple_of(e * 128, 128), 128)
        for v, ref in enumerate((x_ref, g_ref)):
            turned = ref[:, lanes].T
            for a in range(pair):
                to_z = (e * pair) // NX
                to_x = lax.rem(e * pair, NX) + a
                for k in range(chunks):
                    row = a * own + k * CC
                    send[to_z, to_x, k, v] = turned[row : row + CC]

    tiles = channels // 128 // HALVES
    for i in range(HALVES):
        blocks[2 * i].wait()
        blocks[2 * i + 1].wait()
        pl.loop(i * tiles, (i + 1) * tiles)(turn)

    pl.semaphore_wait(barrier, nz + NX + groups - 3)

    def start(source, target, first, second, peer):
        pltpu.make_async_remote_copy(
            src_ref=source, dst_ref=target, send_sem=first, recv_sem=second,
            device_id=peer, device_id_type=MESH,
        ).start()

    for k in range(chunks):
        for r in range(1, NX):
            start(
                send.at[:, round_x[r], k], relay.at[k, :, :, NX - r], send_sem.at[k], relay_sem.at[k], peers_x[r]
            )
        for r in range(1, nz):
            start(
                send.at[round_z[r], x, k], recv.at[k, :, z, 0], send_sem.at[chunks + k], recv_sem.at[k], peers_z[r]
            )

    for k in range(chunks):
        recv[k, :, z, 0] = send[z, x, k]

    def forward(k):
        landed = relay.at[k, :, :, 1:]
        pltpu.make_async_copy(landed, landed, relay_sem.at[k]).wait()
        for r in range(1, nz):
            start(
                relay.at[k, round_z[r], :, 1:], recv.at[k, :, z, 1:], send_sem.at[2 * chunks + k], recv_sem.at[k],
                peers_z[r],
            )
        recv[k, :, z, 1:] = relay[k, z, :, 1:]

    for load in loads:
        load.wait()
    width = 512
    top = 256 - own
    wf = jnp.concatenate([wf_ref[...], jnp.zeros((FP - order, hidden), F32)], axis=0)
    wf_high, wf_low = halves(wf)
    wf_stack = jnp.concatenate([wf_high, wf_high, wf_low], axis=0).T.astype(BF)
    wm_high, wm_low = halves(wm_ref[...])
    wm_stack = jnp.concatenate([wm_high.T, wm_high.T, wm_low.T], axis=0).T.astype(BF)
    first_bias = column(bf_ref[...].reshape(1, hidden))
    second_bias = column(bm_ref[...].reshape(1, hidden))
    odd = lax.rem(ctx, pair) == 1
    rates = rate_ref[lanes_own].reshape(1, 128)
    rates = jnp.where(odd, pltpu.roll(jnp.broadcast_to(rates, (8, 128)), own, 1)[:1], rates)
    decay = column(rates[:, :own])
    wide[hidden : hidden + FP] = feats_ref[:FP]
    wide[hidden + FP : 128] = jnp.zeros((128 - hidden - FP, seq), BF)
    wide[128 : 128 + FP] = feats_ref[FP:]
    wide[128 + FP : top] = jnp.zeros((top - 128 - FP, seq), BF)

    def network(i):
        at = pl.ds(pl.multiple_of(i * width, width), width)
        high = feats_ref[:FP, at]
        stack = jnp.concatenate([high, feats_ref[FP:, at], high], axis=0)
        first, cos_one = sin_cos(mm(wf_stack, stack) + first_bias)
        cos_first[:, at] = cos_one
        high, low = halves(first)
        high, low = high.astype(BF), low.astype(BF)
        wide[:hidden, at] = high
        stack = jnp.concatenate([high, low, high], axis=0)
        second, cos_two = sin_cos(mm(wm_stack, stack) + second_bias)
        act_second[:, at] = second.astype(BF)
        cos_second[:, at] = cos_two
        places = (i * width + lax.broadcasted_iota(jnp.int32, (1, width), 1)).astype(F32)
        modul[:, at] = jnp.exp(-(decay * places) / seq)

    steps = seq // width
    pl.loop(0, steps * 3 // 4)(network)
    forward(0)
    pl.loop(steps * 3 // 4, steps)(network)
    for k in range(1, chunks):
        forward(k)

    def transform(k):
        landed = recv.at[k, :, : nz - 1]
        pltpu.make_async_copy(landed, landed, recv_sem.at[k]).wait()
        turn_re = tw_ref[0][:, None, :]
        turn_im = tw_ref[1][:, None, :]
        for v in range(2):
            columns = [
                recv[k, v, :, behind(t, x, NX)].reshape(nz * CC, FB) for t in range(NX)
            ]
            part_all = mm(fwd_ref[...], jnp.concatenate(columns, axis=0))
            part_re = part_all[: half * CC].reshape(half, CC, FB)
            part_im = part_all[half * CC :].reshape(half, CC, FB)
            spec[:, v, :, :FB] = (part_re * turn_re - part_im * turn_im).astype(BF)
            spec[:, v, :, FB:] = (part_re * turn_im + part_im * turn_re).astype(BF)
        both = mm(spec[...].reshape(half * 2 * CC, 2 * FB), ef_ref[...]).reshape(half, 2, CC, 2 * FB)
        x_re, x_im = both[:, 0, :, :FB], both[:, 0, :, FB:]
        g_re, g_im = both[:, 1, :, :FB], both[:, 1, :, FB:]
        cross = jnp.concatenate(
            [(x_re * g_re + x_im * g_im).astype(BF), (x_re * g_im - x_im * g_re).astype(BF)], axis=-1
        )
        inner = mm(cross.reshape(half * CC, 2 * FB), ei_ref[...]).reshape(half, CC, 2 * FB)
        in_re, in_im = inner[:, :, :FB], inner[:, :, FB:]
        back[:half] = (in_re * turn_re + in_im * turn_im).astype(BF)
        back[half:] = (in_im * turn_re - in_re * turn_im)[1:parts].astype(BF)
        grad = mm(inv_ref[...], back[...].reshape(2 * parts * CC, FB))
        first_row = k * CC if isinstance(k, int) else pl.multiple_of(k * CC, CC)
        for s in range(parts):
            at = slice(s * FB, (s + 1) * FB)
            wide[pl.ds(top + first_row, CC), at] = (
                grad[s * CC : (s + 1) * CC] * modul[pl.ds(first_row, CC), at]
            ).astype(BF)

    pl.loop(0, chunks - 1)(transform)
    transform(chunks - 1)

    span = SPAN
    tile = jnp.where(odd, pltpu.roll(wl_ref[...], own, 1), wl_ref[...])[:, :own]
    high, low = halves(tile.T)
    wl_stack = jnp.concatenate([high, low], axis=0).T.astype(BF)
    wmt_stack = jnp.concatenate([wm_high, wm_low], axis=0).T.astype(BF)
    total = jnp.zeros((3 * hidden, 256), F32)
    for i in range(seq // span):
        at = slice(i * span, (i + 1) * span)
        sh = wide[top:, at]
        d_second = (mm(wl_stack, jnp.concatenate([sh, sh], axis=0)) * cos_second[:, at]).astype(BF)
        d_first = (
            mm(wmt_stack, jnp.concatenate([d_second, d_second], axis=0)) * cos_first[:, at]
        ).astype(BF)
        lines = jnp.concatenate([d_second, d_first, act_second[:, at]], axis=0)
        total = total + nt(lines, wide[:, at])

    rows = hidden // groups
    lane = lax.broadcasted_iota(jnp.int32, (hidden, 128), 1)
    by_second, by_first = total[:hidden], total[hidden : 2 * hidden]
    at_bias = hidden + order
    mixed = by_first[:, :128] + pltpu.roll(by_first[:, 128:], hidden, 1)
    mixed = jnp.where(lane < hidden, by_second[:, :128], mixed)
    mixed = jnp.where(lane == at_bias + 1, pltpu.roll(by_second[:, :128], 1, 1), mixed)
    mixed = jnp.where(lane > at_bias + 1, 0.0, mixed)
    last = total[2 * hidden :, 128:]
    last = jnp.where(odd, last, pltpu.roll(last, own, 1))
    part[:, :rows] = last.reshape(groups, rows, 128)
    part[:, rows:] = mixed.reshape(groups, rows, 128)

    def wait(ref, which):
        pltpu.make_async_copy(ref, ref, sems.at[which]).wait()

    for r in range(1, groups):
        start(part.at[round_dp[r]], got.at[groups - r], sems.at[0], sems.at[1], peers_dp[r])
    wait(got.at[1:groups], 1)
    summed = part[dp]
    for r in range(1, groups):
        summed = summed + got[r]
    ring[0] = summed.astype(BF)

    for r in range(1, parts):
        start(ring.at[0], ring.at[parts - r], sems.at[2], sems.at[3], {"ctx": ahead(ctx, r, parts)})
    wait(ring.at[1:parts], 3)
    low_lanes = lax.broadcasted_iota(jnp.int32, (rows, 128), 1) < own
    summed = jnp.zeros((rows, 128), F32)
    for t in range(0, parts, 2):
        one = ring[behind(t, ctx, parts)].astype(F32)
        two = ring[behind(t + 1, ctx, parts)].astype(F32)
        fin[dp, :, t * own : t * own + 128] = jnp.where(low_lanes, one[:rows], two[:rows]).astype(BF)
        summed = summed + (one[rows:] + two[rows:])
    small[dp] = summed

    for r in range(1, groups):
        start(fin.at[dp], fin.at[dp], sems.at[4], sems.at[5], peers_dp[r])
        start(small.at[dp], small.at[dp], sems.at[6], sems.at[7], peers_dp[r])
    wait(fin.at[: groups - 1], 5)
    wait(small.at[: groups - 1], 7)
    results = [
        pltpu.make_async_copy(source, target, result_sem.at[i])
        for i, (source, target) in enumerate(((fin, last_ref), (small, small_ref)))
    ]
    for result in results:
        result.start()

    wait(got.at[1:groups], 0)
    wait(ring.at[1:parts], 2)
    wait(fin.at[: groups - 1], 4)
    wait(small.at[: groups - 1], 6)
    for k in range(chunks):
        for i, ref in enumerate((relay.at[k, :, :, 1:], recv.at[k, :, : nz - 1, 0], recv.at[k, :, : nz - 1, 1:])):
            pltpu.make_async_copy(ref, ref, send_sem.at[i * chunks + k]).wait()
    for result in results:
        result.wait()


def clip_kernel(count, last_in, small_in, first_ref, first_bias_ref, mid_ref, mid_bias_ref, last_ref):
    groups, rows, channels = last_in.shape
    hidden = groups * rows
    order = first_ref.shape[0]
    grads = last_in[...].astype(F32)
    others = small_in[...].reshape(hidden, 128)
    squares = jnp.sum(jnp.sum(grads * grads, axis=0), keepdims=True) + jnp.sum(others * others, keepdims=True)
    factor = jnp.minimum(1.0, math.sqrt(count) / (jnp.sqrt(squares) + 1e-06))
    last_ref[...] = grads.reshape(hidden, channels) * factor
    others = others * factor
    mid_ref[...] = others[:, :hidden]
    turned = others.T
    first_ref[...] = turned[hidden : hidden + order]
    first_bias_ref[...] = turned[hidden + order]
    mid_bias_ref[...] = turned[hidden + order + 1]


def on_device(inputs, grad_out, w_first, b_first, w_mid, b_mid, w_last, decay_rate):
    parts = lax.axis_size("ctx")
    groups = lax.axis_size("dp")
    channels = inputs.shape[2]
    hidden, order = w_first.shape
    own = channels // parts
    chunks = own // CC
    half = parts + 1
    seq = parts * FB
    rows = hidden // groups
    nz = parts // NX
    tables = make_tables(parts)
    vmem = pl.BlockSpec(memory_space=pltpu.VMEM)
    anywhere = pl.BlockSpec(memory_space=pl.ANY)
    last, small = pl.pallas_call(
        functools.partial(main_kernel, parts, groups),
        out_shape=(
            jax.ShapeDtypeStruct((groups, rows, channels), BF),
            jax.ShapeDtypeStruct((groups, rows, 128), F32),
        ),
        in_specs=[anywhere] * 14,
        out_specs=(anywhere, anywhere),
        scratch_shapes=[
            pltpu.VMEM((FB, channels), BF),
            pltpu.VMEM((FB, channels), BF),
            *(pltpu.VMEM(table.shape, table.dtype) for table in tables),
            pltpu.VMEM((hidden, 128), F32),
            pltpu.VMEM((order, hidden), F32),
            pltpu.VMEM((hidden,), F32),
            pltpu.VMEM((hidden, hidden), F32),
            pltpu.VMEM((hidden,), F32),
            pltpu.VMEM((channels,), F32),
            pltpu.VMEM((nz, NX, chunks, 2, CC, FB), BF),
            pltpu.VMEM((chunks, nz, 2, NX, CC, FB), BF),
            pltpu.VMEM((chunks, 2, nz, NX, CC, FB), BF),
            pltpu.VMEM((half, 2, CC, 2 * FB), BF),
            pltpu.VMEM((2 * parts, CC, FB), BF),
            pltpu.VMEM((hidden, seq), F32),
            pltpu.VMEM((hidden, seq), BF),
            pltpu.VMEM((hidden, seq), F32),
            pltpu.VMEM((256, seq), BF),
            pltpu.VMEM((own, seq), F32),
            pltpu.VMEM((groups, 2 * rows, 128), F32),
            pltpu.VMEM((groups, 2 * rows, 128), F32),
            pltpu.VMEM((parts, 2 * rows, 128), BF),
            pltpu.VMEM((groups, rows, channels), BF),
            pltpu.VMEM((groups, rows, 128), F32),
            pltpu.SemaphoreType.DMA((2 * HALVES,)),
            pltpu.SemaphoreType.DMA((12,)),
            pltpu.SemaphoreType.DMA((3 * chunks,)),
            pltpu.SemaphoreType.DMA((chunks,)),
            pltpu.SemaphoreType.DMA((chunks,)),
            pltpu.SemaphoreType.DMA((8,)),
            pltpu.SemaphoreType.DMA((2,)),
        ],
        compiler_params=pltpu.CompilerParams(
            collective_id=0, has_side_effects=True, vmem_limit_bytes=60 * 1024 * 1024
        ),
    )(
        inputs[0], grad_out[0], *tables, w_last.T,
        w_first.T, b_first, w_mid, b_mid, decay_rate,
    )
    count = hidden * (order + hidden + 2) + channels * hidden
    first, first_bias, mid, mid_bias, last = pl.pallas_call(
        functools.partial(clip_kernel, count),
        out_shape=(
            jax.ShapeDtypeStruct((order, hidden), F32),
            jax.ShapeDtypeStruct((hidden,), F32),
            jax.ShapeDtypeStruct((hidden, hidden), F32),
            jax.ShapeDtypeStruct((hidden,), F32),
            jax.ShapeDtypeStruct((hidden, channels), F32),
        ),
        in_specs=[vmem] * 2,
        out_specs=(vmem,) * 5,
    )(last, small)
    return (first.T, first_bias, mid, mid_bias, last.T)


def solution(mesh):
    in_specs = (P("dp", "ctx", None), P("dp", "ctx", None), P(), P(), P(), P(), P(), P())
    out_specs = (P(), P(), P(), P(), P())
    return jax.shard_map(
        on_device, mesh=mesh, in_specs=in_specs, out_specs=out_specs, check_vma=False
    )
```
